768 devices in a mesh: dp: 96 (over z, x, core), tensor: 8 (over y).
Axes of the slice: x: 4, y: 8, z: 12, core: 2. Of those that a mesh axis runs over, the one named last changes fastest.
Arguments:
- activations: bfloat16 [1152, 40, 3840], P('dp', 'tensor'), may hold values from -6 to 6
- cotangent: bfloat16 [1152, 40, 3584], P('dp', None, 'tensor'), may hold values from -6 to 6
- scales: float32 [576], replicated, may hold values from 0.25 to 4
- slot_worker: int32 [1152], P('dp'), may hold values from 0 to 575, as said below
- slot_counts: int32 [96], replicated, may hold values from 0 to 12, as said below
- owned_block: int32 [96], replicated, may hold values from 0 to 95, each once
Outputs:
- owner_grad: float32 [3840, 3584], P('dp', 'tensor')
The draws below stay inside these ranges and needn't reach their ends.
Inputs may be any that keep to these rules, and one draw needn't show every extreme that they name: `slot_counts`: each dp index has 12 slots; the counts sum to 576, and some dp index holds exactly 12 live slots. `slot_worker`: the live slots, over all dp indices, hold every virtual worker exactly once; slots beyond a dp index's count hold arbitrary ids.
All inputs are finite; a program needn't handle non-finite values.
Results may differ from the reference program's by a relative error of at most 0.0029.
Values may be sent and summed in bfloat16 or wider, within the bound.
No kernel may reach another device: no remote copies, remote signals or barrier semaphores. Data moves between devices by JAX's collectives and lax.ppermute only.
A program may use at most 64 MiB of HBM per device.

```python
import math
import jax
import jax.numpy as jnp
from jax import lax

D_WIN = 3584
MB = 40
VW_DEV = 6
CAP = 12
VIRTUAL = 576
F_W = 3840
BLK = 40
N_DP = 96


def layout_tables(key):
    pair_key, pick_key, order_key, filler_key = jax.random.split(key, 4)
    half_count = N_DP // 2
    shifts = jax.random.randint(pair_key, (half_count,), -(VW_DEV - 1), VW_DEV)
    chosen = jax.random.randint(pick_key, (), 0, half_count)
    shifts = jnp.where(jnp.arange(half_count) == chosen, VW_DEV, shifts)
    counts = jnp.stack([VW_DEV + shifts, VW_DEV - shifts], 1).reshape(N_DP)
    offsets = jnp.cumsum(counts) - counts
    order = jax.random.permutation(order_key, VIRTUAL)
    slot_index = jnp.arange(CAP)
    where_from = jnp.minimum(offsets[:, None] + slot_index[None, :], VIRTUAL - 1)
    live_ids = order[where_from]
    filler = jax.random.randint(filler_key, (N_DP, CAP), 0, VIRTUAL)
    workers = jnp.where(slot_index[None, :] < counts[:, None], live_ids, filler)
    return (workers.reshape(N_DP * CAP).astype(jnp.int32), counts.astype(jnp.int32))


def draw_slot_worker(key, part):
    return layout_tables(key)[0]


def draw_slot_counts(key, part):
    return layout_tables(key)[1]


def level_of(own_key, dims, shards, low, largest):
    def one(axis_at, blocks):
        heights = jax.random.uniform(jax.random.fold_in(jax.random.fold_in(own_key, 6), axis_at), (blocks,), jnp.float32, low / len(shards), largest / len(shards))
        return jnp.repeat(jnp.exp(heights), dims[axis_at] // blocks).reshape((-1,) + (1,) * (len(dims) - axis_at - 1))

    level = one(*shards[0])
    for cut in shards[1:]:
        level = level * one(*cut)
    return level


def normal_values(stream_key, shape, deviation, most, cuts=(), kind=jnp.bfloat16):
    entries = jax.random.normal(stream_key, shape, jnp.float32) * deviation
    if len(cuts) > 0:
        entries = level_of(stream_key, shape, cuts, -0.22, 0.18) * entries
    return jnp.clip(entries, min=-most, max=most).astype(kind)


def setup_inputs(seed: int = 0) -> dict:
    streams_of = jax.random.split(jax.random.key(seed), 7)
    return {
        "activations": normal_values(streams_of[0], (N_DP * CAP, MB, F_W), 1.0, 6.0, ((0, 96), (1, 8))),
        "cotangent": normal_values(streams_of[1], (N_DP * CAP, MB, D_WIN), 1.0, 6.0, ((0, 96), (2, 8))),
        "scales": jnp.clip(jnp.exp(jax.random.uniform(streams_of[2], (VIRTUAL,), jnp.float32, math.log(0.25), math.log(4.0))), 0.25, 4.0),
        "slot_worker": draw_slot_worker(jax.random.fold_in(streams_of[6], 71), 0),
        "slot_counts": draw_slot_counts(jax.random.fold_in(streams_of[6], 71), 0),
        "owned_block": jax.random.permutation(streams_of[5], N_DP).astype(jnp.int32),
    }


def reference(activations, cotangent, scales, slot_worker, slot_counts, owned_block):
    total_slots = activations.shape[0]
    position = jnp.arange(total_slots, dtype=jnp.int32)
    live = (position % CAP) < jnp.repeat(slot_counts, CAP)
    live_weight = jnp.where(live, scales[slot_worker], jnp.zeros((), scales.dtype)) / VIRTUAL
    scaled = (live_weight[:, None, None] * cotangent.astype(jnp.float32)).astype(jnp.bfloat16)

    def add_group(total, group):
        left, right = group
        return total + jnp.einsum("srf,src->fc", left.astype(jnp.float32), right.astype(jnp.float32)), None

    left_groups = activations.reshape(N_DP, CAP, MB, F_W)
    right_groups = scaled.reshape(N_DP, CAP, MB, D_WIN)
    start = jnp.zeros((F_W, D_WIN), jnp.float32)
    weight_grad, unused = lax.scan(add_group, start, (left_groups, right_groups))
    blocks = weight_grad.reshape(N_DP, BLK, D_WIN)[owned_block]
    return blocks.reshape(F_W, D_WIN)
```

```python
import jax
import jax.numpy as jnp
from jax import lax
from jax.experimental import pallas as pl
from jax.experimental.pallas import tpu as pltpu
from jax.sharding import Mesh, PartitionSpec as P

X, C, Y = 4, 2, 8
CAP = 12
ROWS = 40
PER = ROWS // Y
BLK = 40
COLS = 448
TOKENS = 64
PADDED = PER * 16
VIRTUAL = 576
RAISE = 64.0
F32, BF16, F16 = jnp.float32, jnp.bfloat16, jnp.float16
VMEM = pl.BlockSpec(memory_space=pltpu.VMEM)
SMEM = pl.BlockSpec(memory_space=pltpu.SMEM)
ANY = pl.BlockSpec(memory_space=pl.ANY)
PARAMS = pltpu.CompilerParams(vmem_limit_bytes=40 * 1024 * 1024)


def iota(shape, axis):
    return lax.broadcasted_iota(jnp.int32, shape, axis)


def steps(value, width, most):
    return sum((value >= width * i).astype(jnp.int32) for i in range(1, most))


def prepare(zs, act_ref, cot_ref, scales_ref, worker_ref, counts_ref, owned_ref, out_ref, scaled_ref):
    groups = -(-zs // 3)
    dp = (lax.axis_index("z") * X + lax.axis_index("x")) * C + lax.axis_index("c")
    count = counts_ref[dp]
    slot = steps(iota((CAP * ROWS, 1), 0), ROWS, CAP)
    weight = jnp.zeros((CAP * ROWS, 1), F32)
    for s in range(CAP):
        looked_up = jnp.where(s < count, scales_ref[worker_ref[s]], 0.0)
        weight = jnp.where(slot == s, looked_up, weight)
    weight = weight / VIRTUAL
    scaled_ref[...] = (weight * cot_ref[...].astype(F32)).astype(BF16)

    lane = iota((CAP, 128), 1)
    last = act_ref.shape[2] // 128 - 2

    def feature_block(f, carry):
        for g in range(groups):
            tiles = [jnp.zeros((CAP, 128), F32) for _ in range(PER)]
            for j in range(min(3, zs - 3 * g)):
                start = owned_ref[(3 * g + j) * X * C + f] * BLK
                tile = jnp.minimum(start // 128, last)
                shift = lax.rem(BLK * j - (start - tile * 128) + 256, 256)
                window = pl.ds(pl.multiple_of(tile * 128, 128), 256)
                keep = (lane >= BLK * j) & (lane < BLK * (j + 1))
                for t in range(PER):
                    rolled = pltpu.roll(act_ref[t, :, window].astype(F32), shift, 1)
                    tiles[t] = jnp.where(keep, rolled[:, :128], tiles[t])
            for t in range(PER):
                full = jnp.concatenate([tiles[t], jnp.zeros((16 - CAP, 128), F32)], 0)
                out_ref[f, 16 * t : 16 * (t + 1), 128 * g : 128 * (g + 1)] = full.astype(BF16)
        return carry

    lax.fori_loop(0, X * C, feature_block, 0)


def pick(codes_out, codes_in):
    return jnp.where(codes_out == codes_in, 1.0, 0.0).astype(BF16)


def compact_act(wave, counts_ref, got_ref, out_ref):
    base = lax.axis_index("z") * X * C
    m = iota((128, 1), 0)
    half = (m >= TOKENS).astype(jnp.int32)
    row = m - TOKENS * half
    t = steps(row, CAP, 6)
    code_out = jnp.where(row < PER * CAP, half * 10000 + t * 100 + row - CAP * t, -2)
    k = iota((1, 4 * PADDED), 1)
    tile = k >> 4
    s = k & 15
    half_in = (tile >= 2 * PER).astype(jnp.int32)
    core = (tile - 2 * PER * half_in >= PER).astype(jnp.int32)
    t_in = tile - 2 * PER * half_in - PER * core
    for p in range(X // 2):
        n = [counts_ref[base + 4 * p + i] for i in range(4)]
        live = jnp.where(
            half_in == 1, jnp.where(core == 1, n[3], n[2]), jnp.where(core == 1, n[1], n[0])
        )
        ahead = core * jnp.where(half_in == 1, n[2], n[0])
        place = s + ahead - CAP * wave
        there = (s < live) & (place >= 0) & (place < CAP)
        code_in = jnp.where(there, half_in * 10000 + t_in * 100 + place, -1)
        got = got_ref[4 * p * PADDED : 4 * (p + 1) * PADDED, :]
        out = lax.dot_general(
            got, pick(code_out, code_in), (((0,), (1,)), ((), ())), preferred_element_type=F32
        )
        out_ref[:, 128 * p : 128 * (p + 1)] = out.astype(BF16)


def compact_cot(wave, counts_ref, own_ref, other_ref, out_ref):
    base = (lax.axis_index("z") * X + lax.axis_index("x")) * C
    me = lax.axis_index("c")
    first = counts_ref[base]
    k = iota((1, CAP * ROWS), 1)
    slot = steps(k, ROWS, CAP)
    row_in = k - ROWS * slot
    codes = []
    for core in (me, 1 - me):
        place = slot + core * first - CAP * wave
        there = (slot < counts_ref[base + core]) & (place >= 0) & (place < CAP)
        codes.append(jnp.where(there, row_in * 100 + place, -1))
    m = iota((2 * TOKENS, 1), 0)
    half = (m >= TOKENS).astype(jnp.int32)
    row = m - TOKENS * half
    t = steps(row, CAP, 6)
    for p in range(Y // 2):
        r = PER * (2 * p + half) + t
        code_out = jnp.where(row < PER * CAP, r * 100 + row - CAP * t, -2)
        out = jnp.dot(pick(code_out, codes[0]), own_ref[...], preferred_element_type=F32)
        out += jnp.dot(pick(code_out, codes[1]), other_ref[...], preferred_element_type=F32)
        out_ref[2 * TOKENS * p : 2 * TOKENS * (p + 1), :] = out.astype(BF16)


def multiply(zs, waves, *refs):
    acts, cots = refs[: 9 * waves], refs[9 * waves : 13 * waves]
    out_ref, act_s, cot_s, total, sems = refs[13 * waves :]
    x, y = lax.axis_index("x"), lax.axis_index("y")
    half = act_s.shape[1] // 2
    for w in range(waves):
        copies = []

        def copy(src, dst):
            one = pltpu.make_async_copy(src, dst, sems.at[len(copies)])
            one.start()
            copies.append(one)

        for k in range(4):
            copy(cots[4 * w + k], cot_s.at[:, lax.rem(x - k + X, X)])
        for k, ref in zip((0, 1, 2, 3, -1, -2, -3), acts[9 * w : 9 * w + 7]):
            copy(ref, act_s.at[lax.rem(y - k + Y, Y)])
        across = lax.rem(y + Y // 2, Y)
        copy(acts[9 * w + 7], act_s.at[across, 0:half])
        copy(acts[9 * w + 8], act_s.at[across, half : 2 * half])
        for one in copies:
            one.wait()
        part = jnp.zeros(total.shape, F32)
        for i in range(Y):
            part += jnp.dot(
                act_s[i], cot_s[i].reshape(X * TOKENS, COLS), preferred_element_type=F32
            )
        if w > 0:
            part += total[...]
        total[...] = part
    for z in range(zs):
        begin = 128 * (z // 3) + BLK * (z % 3)
        out_ref[z] = total[begin : begin + BLK, :] * RAISE


def body(activations, cotangent, scales, slot_worker, slot_counts, owned_block):
    zs = lax.axis_size("z")
    features = 128 * (-(-zs // 3))
    shape = jax.ShapeDtypeStruct
    act = jnp.transpose(activations, (1, 0, 2))
    cot = cotangent.reshape(CAP * ROWS, COLS)
    sent, scaled = pl.pallas_call(
        lambda *refs: prepare(zs, *refs),
        out_shape=(shape((X * C, PADDED, features), BF16), shape(cot.shape, BF16)),
        in_specs=[VMEM, VMEM, SMEM, SMEM, SMEM, SMEM],
        out_specs=(VMEM, VMEM),
        compiler_params=PARAMS,
    )(act, cot, scales, slot_worker, slot_counts, owned_block)
    other = lax.ppermute(scaled, "c", [(0, 1), (1, 0)])
    got = lax.all_to_all(sent.reshape(X * C * PADDED, features), ("x", "c"), 0, 0, tiled=True)

    def shifted(array, axis, size, by):
        return lax.ppermute(array, axis, [(i, (i + by) % size) for i in range(size)])

    def gathered(wave):
        unit = pl.pallas_call(
            lambda *refs: compact_act(wave, *refs),
            out_shape=shape((features, X * TOKENS), BF16),
            in_specs=[SMEM, VMEM],
            out_specs=VMEM,
            compiler_params=PARAMS,
        )(slot_counts, got)
        chip = pl.pallas_call(
            lambda *refs: compact_cot(wave, *refs),
            out_shape=shape((Y * TOKENS, COLS), BF16),
            in_specs=[SMEM, VMEM, VMEM],
            out_specs=VMEM,
            compiler_params=PARAMS,
        )(slot_counts, scaled, other)
        right, left = [unit], [unit]
        for _ in range(3):
            right.append(shifted(right[-1], "y", Y, 1))
            left.append(shifted(left[-1], "y", Y, -1))
        half = features // 2
        far = [shifted(right[-1][:half], "y", Y, 1), shifted(left[-1][half:], "y", Y, -1)]
        cots = [chip] + [shifted(chip, "x", X, k) for k in (1, 2, 3)]
        return right + left[1:] + far, [c.reshape(Y, TOKENS, COLS) for c in cots]

    def product(*waves):
        acts = [a for wave in waves for a in wave[0]]
        cots = [c for wave in waves for c in wave[1]]
        return pl.pallas_call(
            lambda *refs: multiply(zs, len(waves), *refs),
            out_shape=shape((zs, BLK, COLS), F32),
            in_specs=[ANY] * (len(acts) + len(cots)),
            out_specs=VMEM,
            scratch_shapes=[
                pltpu.VMEM((Y, features, X * TOKENS), BF16),
                pltpu.VMEM((Y, X, TOKENS, COLS), BF16),
                pltpu.VMEM((features, COLS), F32),
                pltpu.SemaphoreType.DMA((13,)),
            ],
            compiler_params=PARAMS,
        )(*acts, *cots).astype(F16)

    first = gathered(0)
    fullest = jnp.max(jnp.sum(slot_counts.reshape(-1, C), axis=1))
    term = lax.cond(
        fullest > CAP, lambda done: product(first, gathered(1)), lambda done: done, product(first)
    )
    parts = lax.all_to_all(term, "z", 0, 0, tiled=True)
    return jnp.sum(parts.astype(F32), axis=0) * (1.0 / RAISE)


def solution(mesh):
    split = Mesh(mesh.devices.reshape(-1, X, C, Y), ("z", "x", "c", "y"))
    dp = ("z", "x", "c")
    return jax.shard_map(
        body,
        mesh=split,
        in_specs=(P(dp, "y", None), P(dp, None, "y"), P(), P(dp), P(), P()),
        out_specs=P(dp, "y"),
        check_vma=False,
    )
```

```python
import jax
import jax.numpy as jnp
from jax import lax
from jax.experimental import pallas as pl
from jax.experimental.pallas import tpu as pltpu
from jax.sharding import Mesh, PartitionSpec as P

X, C, Y = 4, 2, 8
CAP = 12
ROWS = 40
PER = ROWS // Y
BLK = 40
COLS = 448
TOKENS = 64
PADDED = PER * 16
VIRTUAL = 576
RAISE = 64.0
F32, BF16, F16 = jnp.float32, jnp.bfloat16, jnp.float16
VMEM = pl.BlockSpec(memory_space=pltpu.VMEM)
SMEM = pl.BlockSpec(memory_space=pltpu.SMEM)
ANY = pl.BlockSpec(memory_space=pl.ANY)
HBM = pl.BlockSpec(memory_space=pltpu.HBM)
PARAMS = pltpu.CompilerParams(vmem_limit_bytes=40 * 1024 * 1024)


def iota(shape, axis):
    return lax.broadcasted_iota(jnp.int32, shape, axis)


def steps(value, width, most):
    return sum((value >= width * i).astype(jnp.int32) for i in range(1, most))


def fetch(pairs, sems):
    copies = [pltpu.make_async_copy(src, dst, sems.at[i]) for i, (src, dst) in enumerate(pairs)]
    for one in copies:
        one.start()
    return copies


def scale(cot_hbm, scales_ref, worker_ref, counts_ref, scaled_ref, cot_ref, scales_s, worker_s, counts_s, sems):
    copies = fetch(
        [
            (scales_ref, scales_s),
            (worker_ref, worker_s),
            (counts_ref, counts_s),
            (cot_hbm, cot_ref),
        ],
        sems,
    )
    dp = (lax.axis_index("z") * X + lax.axis_index("x")) * C + lax.axis_index("c")
    slot = steps(iota((CAP * ROWS, 1), 0), ROWS, CAP)
    weight = jnp.zeros((CAP * ROWS, 1), F32)
    for one in copies:
        one.wait()
    count = counts_s[dp]
    for s in range(CAP):
        looked_up = jnp.where(s < count, scales_s[worker_s[s]], 0.0)
        weight = jnp.where(slot == s, looked_up, weight)
    weight = weight / VIRTUAL
    scaled_ref[...] = (weight * cot_ref[...].astype(F32)).astype(BF16)


def arrange(zs, act_ref, owned_ref, out_ref, owned_s, sems):
    copies = fetch([(owned_ref, owned_s)], sems)
    groups = -(-zs // 3)
    lane = iota((CAP, 128), 1)
    last = act_ref.shape[2] // 128 - 2
    for one in copies:
        one.wait()

    def feature_block(f, carry):
        for g in range(groups):
            tiles = [jnp.zeros((CAP, 128), F32) for _ in range(PER)]
            for j in range(min(3, zs - 3 * g)):
                start = owned_s[(3 * g + j) * X * C + f] * BLK
                tile = jnp.minimum(start // 128, last)
                shift = lax.rem(BLK * j - (start - tile * 128) + 256, 256)
                window = pl.ds(pl.multiple_of(tile * 128, 128), 256)
                keep = (lane >= BLK * j) & (lane < BLK * (j + 1))
                for t in range(PER):
                    rolled = pltpu.roll(act_ref[t, :, window].astype(F32), shift, 1)
                    tiles[t] = jnp.where(keep, rolled[:, :128], tiles[t])
            for t in range(PER):
                full = jnp.concatenate([tiles[t], jnp.zeros((16 - CAP, 128), F32)], 0)
                out_ref[f, 16 * t : 16 * (t + 1), 128 * g : 128 * (g + 1)] = full.astype(BF16)
        return carry

    lax.fori_loop(0, X * C, feature_block, 0)


def pick(codes_out, codes_in):
    return jnp.where(codes_out == codes_in, 1.0, 0.0).astype(BF16)


def compact_act(wave, counts_hbm, got_ref, one_ref, two_ref, out_ref, *rest):
    counts_ref, sems = rest[2:]
    copies = fetch([(counts_hbm, counts_ref)], sems)
    base = lax.axis_index("z") * X * C
    m = iota((128, 1), 0)
    half = (m >= TOKENS).astype(jnp.int32)
    row = m - TOKENS * half
    t = steps(row, CAP, 6)
    code_out = jnp.where(row < PER * CAP, half * 10000 + t * 100 + row - CAP * t, -2)
    k = iota((1, 4 * PADDED), 1)
    tile = k >> 4
    s = k & 15
    half_in = (tile >= 2 * PER).astype(jnp.int32)
    core = (tile - 2 * PER * half_in >= PER).astype(jnp.int32)
    t_in = tile - 2 * PER * half_in - PER * core
    for one in copies:
        one.wait()
    for p in range(X // 2):
        n = [counts_ref[base + 4 * p + i] for i in range(4)]
        live = jnp.where(
            half_in == 1, jnp.where(core == 1, n[3], n[2]), jnp.where(core == 1, n[1], n[0])
        )
        ahead = core * jnp.where(half_in == 1, n[2], n[0])
        place = s + ahead - CAP * wave
        there = (s < live) & (place >= 0) & (place < CAP)
        code_in = jnp.where(there, half_in * 10000 + t_in * 100 + place, -1)
        got = got_ref[4 * p * PADDED : 4 * (p + 1) * PADDED, :]
        out = lax.dot_general(
            got, pick(code_out, code_in), (((0,), (1,)), ((), ())), preferred_element_type=F32
        )
        out_ref[:, 128 * p : 128 * (p + 1)] = out.astype(BF16)


def compact_cot(wave, counts_hbm, own_ref, other_ref, passed_ref, out_ref, same_ref, counts_ref, sems):
    copies = fetch([(counts_hbm, counts_ref)], sems)
    base = (lax.axis_index("z") * X + lax.axis_index("x")) * C
    me = lax.axis_index("c")
    for one in copies:
        one.wait()
    first = counts_ref[base]
    k = iota((1, CAP * ROWS), 1)
    slot = steps(k, ROWS, CAP)
    row_in = k - ROWS * slot
    codes = []
    for core in (me, 1 - me):
        place = slot + core * first - CAP * wave
        there = (slot < counts_ref[base + core]) & (place >= 0) & (place < CAP)
        codes.append(jnp.where(there, row_in * 100 + place, -1))
    m = iota((2 * TOKENS, 1), 0)
    half = (m >= TOKENS).astype(jnp.int32)
    row = m - TOKENS * half
    t = steps(row, CAP, 6)
    for p in range(Y // 2):
        r = PER * (2 * p + half) + t
        code_out = jnp.where(row < PER * CAP, r * 100 + row - CAP * t, -2)
        out = jnp.dot(pick(code_out, codes[0]), own_ref[...], preferred_element_type=F32)
        out += jnp.dot(pick(code_out, codes[1]), other_ref[...], preferred_element_type=F32)
        out_ref[2 * TOKENS * p : 2 * TOKENS * (p + 1), :] = out.astype(BF16)


def multiply(zs, waves, *refs):
    acts, cots = refs[: 8 * waves], refs[8 * waves : 12 * waves]
    out_ref, cot_s, total, sems = refs[12 * waves :]
    x, y = lax.axis_index("x"), lax.axis_index("y")
    sign = 1 - 2 * lax.axis_index("c")
    for w in range(waves):
        places = [
            (ref, cot_s.at[:, lax.rem(x - sign * k + X, X)])
            for k, ref in zip((0, 1, -1, 2), cots[4 * w : 4 * w + 4])
        ]
        for copy in fetch(places, sems):
            copy.wait()
        part = jnp.zeros(total.shape, F32)
        for k, ref in zip((0, 1, -1, 2, -2, 3, -3, 4), acts[8 * w : 8 * w + 8]):
            cot = cot_s[lax.rem(y - sign * k + Y, Y)].reshape(X * TOKENS, COLS)
            part += jnp.dot(ref[...], cot, preferred_element_type=F32)
        if w > 0:
            part += total[...]
        total[...] = part
    for z in range(zs):
        begin = 128 * (z // 3) + BLK * (z % 3)
        out_ref[z] = total[begin : begin + BLK, :] * RAISE


def body(activations, cotangent, scales, slot_worker, slot_counts, owned_block):
    zs = lax.axis_size("z")
    features = 128 * (-(-zs // 3))
    shape = jax.ShapeDtypeStruct
    act = jnp.transpose(activations, (1, 0, 2))
    cot = cotangent.reshape(CAP * ROWS, COLS)
    ids = jnp.int32
    scaled = pl.pallas_call(
        scale,
        out_shape=shape(cot.shape, BF16),
        in_specs=[HBM, HBM, HBM, HBM],
        out_specs=VMEM,
        scratch_shapes=[
            pltpu.VMEM(cot.shape, BF16),
            pltpu.SMEM(scales.shape, F32),
            pltpu.SMEM(slot_worker.shape, ids),
            pltpu.SMEM(slot_counts.shape, ids),
            pltpu.SemaphoreType.DMA((4,)),
        ],
        compiler_params=PARAMS,
    )(cot, scales, slot_worker, slot_counts)
    other = lax.ppermute(scaled, "c", [(0, 1), (1, 0)])
    sent = pl.pallas_call(
        lambda *refs: arrange(zs, *refs),
        out_shape=shape((X * C, PADDED, features), BF16),
        in_specs=[VMEM, HBM],
        out_specs=VMEM,
        scratch_shapes=[pltpu.SMEM(owned_block.shape, ids), pltpu.SemaphoreType.DMA((1,))],
        compiler_params=PARAMS,
    )(act, owned_block)

    counts_scratch = [pltpu.SMEM(slot_counts.shape, ids), pltpu.SemaphoreType.DMA((1,))]

    def chip_cot(wave, passed):
        return pl.pallas_call(
            lambda *refs: compact_cot(wave, *refs),
            out_shape=(shape((Y * TOKENS, COLS), BF16), shape(passed.shape, passed.dtype)),
            in_specs=[HBM, VMEM, VMEM, ANY],
            out_specs=(VMEM, ANY),
            scratch_shapes=counts_scratch,
            input_output_aliases={3: 1},
            compiler_params=PARAMS,
        )(slot_counts, scaled, other, passed)

    chip, sent = chip_cot(0, sent)

    def shifted(array, axis, size, by):
        names = ("x", "c") if axis == "x" else ("c", axis)
        number = lambda c, i: i * C + c if axis == "x" else c * size + i
        pairs = [
            (number(c, i), number(c, (i + by * (1 - 2 * c)) % size))
            for c in range(C)
            for i in range(size)
        ]
        return lax.ppermute(array, names, pairs)

    def gathered(wave, chip, got, one, two):
        unit, one, two = pl.pallas_call(
            lambda *refs: compact_act(wave, *refs),
            out_shape=(
                shape((features, X * TOKENS), BF16),
                shape(chip.shape, BF16),
                shape(chip.shape, BF16),
            ),
            in_specs=[HBM, VMEM, ANY, ANY],
            out_specs=(VMEM, ANY, ANY),
            scratch_shapes=counts_scratch,
            input_output_aliases={2: 1, 3: 2},
            compiler_params=PARAMS,
        )(slot_counts, got, one, two)
        near = [shifted(unit, "y", Y, 1), shifted(unit, "y", Y, -1)]
        ahead, behind = shifted(unit, "y", Y, 2), shifted(unit, "y", Y, -2)
        far = [shifted(ahead, "y", Y, 1), shifted(behind, "y", Y, -1), shifted(ahead, "y", Y, 2)]
        cots = [chip, one, two, shifted(one, "x", X, 1)]
        return [unit, *near, ahead, behind, *far], [c.reshape(Y, TOKENS, COLS) for c in cots]

    def beside(chip):
        return shifted(chip, "x", X, 1), shifted(chip, "x", X, -1)

    def product(*waves):
        acts = [a for wave in waves for a in wave[0]]
        cots = [c for wave in waves for c in wave[1]]
        return pl.pallas_call(
            lambda *refs: multiply(zs, len(waves), *refs),
            out_shape=shape((zs, BLK, COLS), F32),
            in_specs=[VMEM] * len(acts) + [ANY] * len(cots),
            out_specs=VMEM,
            scratch_shapes=[
                pltpu.VMEM((Y, X, TOKENS, COLS), BF16),
                pltpu.VMEM((features, COLS), F32),
                pltpu.SemaphoreType.DMA((4,)),
            ],
            compiler_params=PARAMS,
        )(*acts, *cots).astype(F16)

    one, two = beside(chip)
    got = lax.all_to_all(sent.reshape(X * C * PADDED, features), ("x", "c"), 0, 0, tiled=True)
    first = gathered(0, chip, got, one, two)
    fullest = jnp.max(jnp.sum(slot_counts.reshape(-1, C), axis=1))

    def more(done):
        again, passed = chip_cot(1, got)
        return product(first, gathered(1, again, passed, *beside(again)))

    term = lax.cond(fullest > CAP, more, lambda done: done, product(first))
    parts = lax.all_to_all(term, "z", 0, 0, tiled=True)
    return jnp.sum(parts.astype(F32), axis=0) * (1.0 / RAISE)


def solution(mesh):
    split = Mesh(mesh.devices.reshape(-1, X, C, Y), ("z", "x", "c", "y"))
    dp = ("z", "x", "c")
    return jax.shard_map(
        body,
        mesh=split,
        in_specs=(P(dp, "y", None), P(dp, None, "y"), P(), P(dp), P(), P()),
        out_specs=P(dp, "y"),
        check_vma=False,
    )
```

```python
import jax
import jax.numpy as jnp
from jax import lax
from jax.experimental import pallas as pl
from jax.experimental.pallas import tpu as pltpu
from jax.sharding import Mesh, PartitionSpec as P

X, C, Y = 4, 2, 8
CAP = 12
ROWS = 40
PER = ROWS // Y
BLK = 40
COLS = 448
LANES = 512
TOKENS = 64
VIRTUAL = 576
RAISE = 64.0
F32, BF16, F16 = jnp.float32, jnp.bfloat16, jnp.float16
VMEM = pl.BlockSpec(memory_space=pltpu.VMEM)
SMEM = pl.BlockSpec(memory_space=pltpu.SMEM)
ANY = pl.BlockSpec(memory_space=pl.ANY)
PARAMS = pltpu.CompilerParams(vmem_limit_bytes=32 * 1024 * 1024)
WIDE = pltpu.CompilerParams(vmem_limit_bytes=60 * 1024 * 1024)


def iota(shape, axis):
    return lax.broadcasted_iota(jnp.int32, shape, axis)


def steps(value, width, most):
    return sum((value >= width * i).astype(jnp.int32) for i in range(1, most))


def fetch(pairs, sems):
    copies = [pltpu.make_async_copy(src, dst, sems.at[i]) for i, (src, dst) in enumerate(pairs)]
    for one in copies:
        one.start()
    return copies


def prepare(zs, *refs):
    sources, (out_ref, scaled_ref), held = refs[:6], refs[6:8], refs[8:14]
    act_ref, cot_ref, scales_ref, worker_ref, counts_ref, owned_ref = held
    copies = fetch(list(zip(sources, held)), refs[14])
    dp = (lax.axis_index("z") * X + lax.axis_index("x")) * C + lax.axis_index("c")
    slot = steps(iota((CAP * ROWS, 1), 0), ROWS, CAP)
    weight = jnp.zeros((CAP * ROWS, 1), F32)
    for one in copies[1:]:
        one.wait()
    count = counts_ref[dp]
    for s in range(CAP):
        looked_up = jnp.where(s < count, scales_ref[worker_ref[s]], 0.0)
        weight = jnp.where(slot == s, looked_up, weight)
    weight = weight / VIRTUAL
    scaled_ref[...] = (weight * cot_ref[...].astype(F32)).astype(BF16)

    groups = -(-zs // 3)
    lane = iota((CAP, 128), 1)
    last = act_ref.shape[2] // 128 - 2
    copies[0].wait()

    def feature_block(f, carry):
        for g in range(groups):
            tiles = [jnp.zeros((CAP, 128), F32) for _ in range(PER)]
            for j in range(min(3, zs - 3 * g)):
                start = owned_ref[(3 * g + j) * X * C + f] * BLK
                tile = jnp.minimum(start // 128, last)
                shift = lax.rem(BLK * j - (start - tile * 128) + 256, 256)
                window = pl.ds(pl.multiple_of(tile * 128, 128), 256)
                keep = (lane >= BLK * j) & (lane < BLK * (j + 1))
                for t in range(PER):
                    rolled = pltpu.roll(act_ref[t, :, window].astype(F32), shift, 1)
                    tiles[t] = jnp.where(keep, rolled[:, :128], tiles[t])
            full = jnp.concatenate([*tiles, jnp.zeros((TOKENS - PER * CAP, 128), F32)], 0)
            out_ref[f, :, 128 * g : 128 * (g + 1)] = full.astype(BF16)
        return carry

    lax.fori_loop(0, X * C, feature_block, 0)


def pick(codes_out, codes_in):
    return jnp.where(codes_out == codes_in, 1.0, 0.0).astype(BF16)


def compact_act(wave, counts_hbm, got_ref, out_ref, counts_ref, sems):
    copies = fetch([(counts_hbm, counts_ref)], sems)
    base = lax.axis_index("z") * X * C
    m = iota((2 * TOKENS, 1), 0)
    half = (m >= TOKENS).astype(jnp.int32)
    row = m - TOKENS * half
    t = steps(row, CAP, 6)
    code_out = jnp.where(row < PER * CAP, half * 10000 + t * 100 + row - CAP * t, -2)
    k = iota((1, 2 * C * TOKENS), 1)
    block = steps(k, TOKENS, 2 * C)
    row = k - TOKENS * block
    t = steps(row, CAP, 6)
    s = row - CAP * t
    half = block >> 1
    core = block & 1
    for one in copies:
        one.wait()
    for p in range(X // 2):
        n = [counts_ref[base + 4 * p + i] for i in range(4)]
        live = jnp.where(
            half == 1, jnp.where(core == 1, n[3], n[2]), jnp.where(core == 1, n[1], n[0])
        )
        place = s + core * jnp.where(half == 1, n[2], n[0]) - CAP * wave
        there = (row < PER * CAP) & (s < live) & (place >= 0) & (place < CAP)
        code_in = jnp.where(there, half * 10000 + t * 100 + place, -1)
        got = got_ref[2 * C * p * TOKENS : 2 * C * (p + 1) * TOKENS, :]
        out = lax.dot_general(
            got, pick(code_out, code_in), (((0,), (1,)), ((), ())), preferred_element_type=F32
        )
        out_ref[:, 128 * p : 128 * (p + 1)] = out.astype(BF16)


def compact_cot(wave, counts_hbm, own_ref, other_ref, out_ref, counts_ref, sems):
    copies = fetch([(counts_hbm, counts_ref)], sems)
    base = (lax.axis_index("z") * X + lax.axis_index("x")) * C
    me = lax.axis_index("c")
    for one in copies:
        one.wait()
    first = counts_ref[base]
    k = iota((1, CAP * ROWS), 1)
    slot = steps(k, ROWS, CAP)
    row_in = k - ROWS * slot
    codes = []
    for core in (me, 1 - me):
        place = slot + core * first - CAP * wave
        there = (slot < counts_ref[base + core]) & (place >= 0) & (place < CAP)
        codes.append(jnp.where(there, row_in * 100 + place, -1))
    m = iota((2 * TOKENS, 1), 0)
    half = (m >= TOKENS).astype(jnp.int32)
    row = m - TOKENS * half
    t = steps(row, CAP, 6)
    for p in range(Y // 2):
        r = PER * (2 * p + half) + t
        code_out = jnp.where(row < PER * CAP, r * 100 + row - CAP * t, -2)
        out = jnp.dot(pick(code_out, codes[0]), own_ref[...], preferred_element_type=F32)
        out += jnp.dot(pick(code_out, codes[1]), other_ref[...], preferred_element_type=F32)
        full = jnp.concatenate([out, jnp.zeros((2 * TOKENS, LANES - COLS), F32)], 1)
        out_ref[2 * TOKENS * p : 2 * TOKENS * (p + 1), :] = full.astype(BF16)


def join(after_ref, one_ref, two_ref, out_ref, sems):
    rows = one_ref.shape[0]
    halves = [(one_ref, out_ref.at[0:rows]), (two_ref, out_ref.at[rows : 2 * rows])]
    for copy in fetch(halves, sems):
        copy.wait()


def multiply(zs, waves, *refs):
    acts, cots = refs[: 8 * waves], refs[8 * waves : 11 * waves]
    out_ref, cot_s, total, sems = refs[11 * waves :]
    x, y, c = lax.axis_index("x"), lax.axis_index("y"), lax.axis_index("c")
    sign = 1 - 2 * c
    near = 1 + 2 * c
    for w in range(waves):
        own, one, pair = cots[3 * w : 3 * w + 3]
        places = [
            (own, cot_s.at[:, x]),
            (one, cot_s.at[:, x ^ near]),
            (pair.at[0:Y], cot_s.at[:, x ^ (4 - near)]),
            (pair.at[Y : 2 * Y], cot_s.at[:, x ^ 2]),
        ]
        for copy in fetch(places, sems):
            copy.wait()
        part = jnp.zeros(total.shape, F32)
        for k, ref in zip((0, 1, -1, 2, -2, 3, -3, 4), acts[8 * w : 8 * w + 8]):
            cot = cot_s[lax.rem(y - sign * k + Y, Y)].reshape(X * TOKENS, LANES)[:, :COLS]
            part += jnp.dot(ref[...], cot, preferred_element_type=F32)
        if w > 0:
            part += total[...]
        total[...] = part
    for z in range(zs):
        begin = 128 * (z // 3) + BLK * (z % 3)
        out_ref[z] = total[begin : begin + BLK, :] * RAISE


def body(activations, cotangent, scales, slot_worker, slot_counts, owned_block):
    zs = lax.axis_size("z")
    features = 128 * (-(-zs // 3))
    shape = jax.ShapeDtypeStruct
    act = jnp.transpose(activations, (1, 0, 2))
    cot = cotangent.reshape(CAP * ROWS, COLS)
    inputs = (act, cot, scales, slot_worker, slot_counts, owned_block)
    sent, scaled = pl.pallas_call(
        lambda *refs: prepare(zs, *refs),
        out_shape=(shape((X * C, TOKENS, features), BF16), shape(cot.shape, BF16)),
        in_specs=[ANY] * 6,
        out_specs=(VMEM, VMEM),
        scratch_shapes=[
            *[pltpu.VMEM(a.shape, a.dtype) for a in inputs[:2]],
            *[pltpu.SMEM(a.shape, a.dtype) for a in inputs[2:]],
            pltpu.SemaphoreType.DMA((6,)),
        ],
        compiler_params=WIDE,
    )(*inputs)
    got = lax.all_to_all(sent.reshape(X * C * TOKENS, features), ("x", "c"), 0, 0, tiled=True)
    other = lax.ppermute(scaled, "c", [(0, 1), (1, 0)])
    counts_scratch = [
        pltpu.SMEM(slot_counts.shape, jnp.int32),
        pltpu.SemaphoreType.DMA((1,)),
    ]

    def shifted(array, by):
        pairs = [
            (c * Y + y, c * Y + (y + by * (1 - 2 * c)) % Y) for c in range(C) for y in range(Y)
        ]
        return lax.ppermute(array, ("c", "y"), pairs)

    def swapped(array, first):
        pairs = [
            (x * C + c, (x ^ (1 if (c == 0) == first else 3)) * C + c)
            for x in range(X)
            for c in range(C)
        ]
        return lax.ppermute(array, ("x", "c"), pairs)

    def gathered(wave):
        unit = pl.pallas_call(
            lambda *refs: compact_act(wave, *refs),
            out_shape=shape((features, X * TOKENS), BF16),
            in_specs=[ANY, VMEM],
            out_specs=VMEM,
            scratch_shapes=counts_scratch,
            compiler_params=PARAMS,
        )(slot_counts, got)
        chip = pl.pallas_call(
            lambda *refs: compact_cot(wave, *refs),
            out_shape=shape((Y * TOKENS, LANES), BF16),
            in_specs=[ANY, VMEM, VMEM],
            out_specs=VMEM,
            scratch_shapes=counts_scratch,
            compiler_params=PARAMS,
        )(slot_counts, scaled, other)
        one = swapped(chip, True)
        both = pl.pallas_call(
            join,
            out_shape=shape((2 * chip.shape[0], LANES), BF16),
            in_specs=[ANY, ANY, ANY],
            out_specs=ANY,
            scratch_shapes=[pltpu.SemaphoreType.DMA((2,))],
            compiler_params=PARAMS,
        )(unit, chip, one)
        pair = swapped(both, False)
        near = [shifted(unit, 1), shifted(unit, -1)]
        ahead, behind = shifted(unit, 2), shifted(unit, -2)
        far = [shifted(ahead, 1), shifted(behind, -1), shifted(ahead, 2)]
        cots = [c.reshape(-1, TOKENS, LANES) for c in (chip, one, pair)]
        return [unit, *near, ahead, behind, *far], cots

    def product(*waves):
        acts = [a for wave in waves for a in wave[0]]
        cots = [c for wave in waves for c in wave[1]]
        return pl.pallas_call(
            lambda *refs: multiply(zs, len(waves), *refs),
            out_shape=shape((zs, BLK, COLS), F32),
            in_specs=[VMEM] * len(acts) + [ANY] * len(cots),
            out_specs=VMEM,
            scratch_shapes=[
                pltpu.VMEM((Y, X, TOKENS, LANES), BF16),
                pltpu.VMEM((features, COLS), F32),
                pltpu.SemaphoreType.DMA((4,)),
            ],
            compiler_params=PARAMS,
        )(*acts, *cots).astype(F16)

    first = gathered(0)
    fullest = jnp.max(jnp.sum(slot_counts.reshape(-1, C), axis=1))
    term = lax.cond(
        fullest > CAP, lambda done: product(first, gathered(1)), lambda done: done, product(first)
    )
    parts = lax.all_to_all(term, "z", 0, 0, tiled=True)
    return jnp.sum(parts.astype(F32), axis=0) * (1.0 / RAISE)


def solution(mesh):
    split = Mesh(mesh.devices.reshape(-1, X, C, Y), ("z", "x", "c", "y"))
    dp = ("z", "x", "c")
    return jax.shard_map(
        body,
        mesh=split,
        in_specs=(P(dp, "y", None), P(dp, None, "y"), P(), P(dp), P(), P()),
        out_specs=P(dp, "y"),
        check_vma=False,
    )
```

```python
import jax
import jax.numpy as jnp
from jax import lax
from jax.experimental import pallas as pl
from jax.experimental.pallas import tpu as pltpu
from jax.sharding import Mesh, PartitionSpec as P

X, C, Y = 4, 2, 8
CAP = 12
ROWS = 40
PER = ROWS // Y
BLK = 40
COLS = 448
LANES = 512
TOKENS = 64
VIRTUAL = 576
RAISE = 64.0
F32, BF16, F16 = jnp.float32, jnp.bfloat16, jnp.float16
VMEM = pl.BlockSpec(memory_space=pltpu.VMEM)
SMEM = pl.BlockSpec(memory_space=pltpu.SMEM)
ANY = pl.BlockSpec(memory_space=pl.ANY)
PARAMS = pltpu.CompilerParams(vmem_limit_bytes=32 * 1024 * 1024)
WIDE = pltpu.CompilerParams(vmem_limit_bytes=56 * 1024 * 1024)


def iota(shape, axis):
    return lax.broadcasted_iota(jnp.int32, shape, axis)


def steps(value, width, most):
    return sum((value >= width * i).astype(jnp.int32) for i in range(1, most))


def fetch(pairs, sems):
    copies = [pltpu.make_async_copy(src, dst, sems.at[i]) for i, (src, dst) in enumerate(pairs)]
    for one in copies:
        one.start()
    return copies


def prepare(zs, *refs):
    sources, (out_ref, scaled_ref), held = refs[:6], refs[6:8], refs[8:14]
    act_ref, cot_ref, scales_ref, worker_ref, counts_ref, owned_ref = held
    copies = fetch(list(zip(sources, held)), refs[14])
    dp = (lax.axis_index("z") * X + lax.axis_index("x")) * C + lax.axis_index("c")
    slot = steps(iota((CAP * ROWS, 1), 0), ROWS, CAP)
    weight = jnp.zeros((CAP * ROWS, 1), F32)
    for one in copies[1:]:
        one.wait()
    count = counts_ref[dp]
    for s in range(CAP):
        looked_up = jnp.where(s < count, scales_ref[worker_ref[s]], 0.0)
        weight = jnp.where(slot == s, looked_up, weight)
    weight = weight / VIRTUAL
    scaled_ref[...] = (weight * cot_ref[...].astype(F32)).astype(BF16)

    groups = -(-zs // 3)
    lane = iota((CAP, 128), 1)
    last = act_ref.shape[2] // 128 - 2
    copies[0].wait()

    def feature_block(f, carry):
        for g in range(groups):
            tiles = [jnp.zeros((CAP, 128), F32) for _ in range(PER)]
            for j in range(min(3, zs - 3 * g)):
                start = owned_ref[(3 * g + j) * X * C + f] * BLK
                tile = jnp.minimum(start // 128, last)
                shift = lax.rem(BLK * j - (start - tile * 128) + 256, 256)
                window = pl.ds(pl.multiple_of(tile * 128, 128), 256)
                keep = (lane >= BLK * j) & (lane < BLK * (j + 1))
                for t in range(PER):
                    rolled = pltpu.roll(act_ref[t, :, window].astype(F32), shift, 1)
                    tiles[t] = jnp.where(keep, rolled[:, :128], tiles[t])
            full = jnp.concatenate([*tiles, jnp.zeros((TOKENS - PER * CAP, 128), F32)], 0)
            out_ref[f, :, 128 * g : 128 * (g + 1)] = full.astype(BF16)
        return carry

    lax.fori_loop(0, X * C, feature_block, 0)


def pick(codes_out, codes_in):
    return jnp.where(codes_out == codes_in, 1.0, 0.0).astype(BF16)


def compact(wave, counts_hbm, got_ref, own_ref, other_ref, unit_ref, chip_ref, counts_ref, sems):
    copies = fetch([(counts_hbm, counts_ref)], sems)
    compact_act(wave, copies, counts_ref, got_ref, unit_ref)
    compact_cot(wave, counts_ref, own_ref, other_ref, chip_ref)


def compact_act(wave, copies, counts_ref, got_ref, out_ref):
    base = lax.axis_index("z") * X * C
    m = iota((2 * TOKENS, 1), 0)
    half = (m >= TOKENS).astype(jnp.int32)
    row = m - TOKENS * half
    t = steps(row, CAP, 6)
    code_out = jnp.where(row < PER * CAP, half * 10000 + t * 100 + row - CAP * t, -2)
    k = iota((1, 2 * C * TOKENS), 1)
    block = steps(k, TOKENS, 2 * C)
    row = k - TOKENS * block
    t = steps(row, CAP, 6)
    s = row - CAP * t
    half = block >> 1
    core = block & 1
    for one in copies:
        one.wait()
    for p in range(X // 2):
        n = [counts_ref[base + 4 * p + i] for i in range(4)]
        live = jnp.where(
            half == 1, jnp.where(core == 1, n[3], n[2]), jnp.where(core == 1, n[1], n[0])
        )
        place = s + core * jnp.where(half == 1, n[2], n[0]) - CAP * wave
        there = (row < PER * CAP) & (s < live) & (place >= 0) & (place < CAP)
        code_in = jnp.where(there, half * 10000 + t * 100 + place, -1)
        got = got_ref[2 * C * p * TOKENS : 2 * C * (p + 1) * TOKENS, :]
        out = lax.dot_general(
            got, pick(code_out, code_in), (((0,), (1,)), ((), ())), preferred_element_type=F32
        )
        out_ref[:, 128 * p : 128 * (p + 1)] = out.astype(BF16)


def compact_cot(wave, counts_ref, own_ref, other_ref, out_ref):
    base = (lax.axis_index("z") * X + lax.axis_index("x")) * C
    me = lax.axis_index("c")
    first = counts_ref[base]
    k = iota((1, CAP * ROWS), 1)
    slot = steps(k, ROWS, CAP)
    row_in = k - ROWS * slot
    codes = []
    for core in (me, 1 - me):
        place = slot + core * first - CAP * wave
        there = (slot < counts_ref[base + core]) & (place >= 0) & (place < CAP)
        codes.append(jnp.where(there, row_in * 100 + place, -1))
    m = iota((2 * TOKENS, 1), 0)
    half = (m >= TOKENS).astype(jnp.int32)
    row = m - TOKENS * half
    t = steps(row, CAP, 6)
    for p in range(Y // 2):
        r = PER * (2 * p + half) + t
        code_out = jnp.where(row < PER * CAP, r * 100 + row - CAP * t, -2)
        out = jnp.dot(pick(code_out, codes[0]), own_ref[...], preferred_element_type=F32)
        out += jnp.dot(pick(code_out, codes[1]), other_ref[...], preferred_element_type=F32)
        full = jnp.concatenate([out, jnp.zeros((2 * TOKENS, LANES - COLS), F32)], 1)
        out_ref[2 * TOKENS * p : 2 * TOKENS * (p + 1), :] = full.astype(BF16)


def multiply_near(begun, *refs):
    acts, cots, rest = refs[:5], refs[5:9], refs[9 + begun :]
    out_ref, cot_ref, sems = rest
    x, y, c = lax.axis_index("x"), lax.axis_index("y"), lax.axis_index("c")
    near = 1 + 2 * c
    places = [
        (ref, cot_ref.at[:, x ^ by]) for ref, by in zip(cots, (0, near, 4 - near, 2))
    ]
    for copy in fetch(places, sems):
        copy.wait()
    total = refs[9][...] if begun else jnp.zeros(out_ref.shape, F32)
    out_ref[...] = total + outer(y, c, acts, (0, 1, -1, 2, -2), cot_ref)


def outer(y, c, acts, ks, cot_ref):
    total = jnp.zeros((acts[0].shape[0], LANES), F32)
    for k, ref in zip(ks, acts):
        cot = cot_ref[lax.rem(y - (1 - 2 * c) * k + Y, Y)].reshape(X * TOKENS, LANES)
        total += jnp.dot(ref[...], cot, preferred_element_type=F32)
    return total


def multiply_far(zs, last, *refs):
    acts, (cot_ref, total_ref, out_ref) = refs[:3], refs[3:]
    y, c = lax.axis_index("y"), lax.axis_index("c")
    total = total_ref[...] + outer(y, c, acts, (3, -3, 4), cot_ref)
    if not last:
        out_ref[...] = total
        return
    for z in range(zs):
        begin = 128 * (z // 3) + BLK * (z % 3)
        out_ref[z] = total[begin : begin + BLK, :COLS] * RAISE


def body(*inputs):
    term = partial_sums(*inputs)
    counts = inputs[4]
    fullest = jnp.max(jnp.sum(counts.reshape(-1, C), axis=1))
    term = lax.cond(
        fullest > CAP, lambda done, *again: partial_sums(*again, waves=C), lambda done, *_: done,
        term, *inputs,
    )
    parts = lax.all_to_all(term, "z", 0, 0, tiled=True)
    return jnp.sum(parts.astype(F32) * (1.0 / RAISE), axis=0)


def partial_sums(
    activations, cotangent, scales, slot_worker, slot_counts, owned_block, waves=1
):
    zs = lax.axis_size("z")
    features = 128 * (-(-zs // 3))
    shape = jax.ShapeDtypeStruct
    act = jnp.transpose(activations, (1, 0, 2))
    cot = cotangent.reshape(CAP * ROWS, COLS)
    inputs = (act, cot, scales, slot_worker, slot_counts, owned_block)
    sent, scaled = pl.pallas_call(
        lambda *refs: prepare(zs, *refs),
        out_shape=(pltpu.VMEM((X * C, TOKENS, features), BF16), pltpu.VMEM(cot.shape, BF16)),
        in_specs=[ANY] * 6,
        out_specs=(VMEM, VMEM),
        scratch_shapes=[
            *[pltpu.VMEM(a.shape, a.dtype) for a in inputs[:2]],
            *[pltpu.SMEM(a.shape, a.dtype) for a in inputs[2:]],
            pltpu.SemaphoreType.DMA((6,)),
        ],
        compiler_params=WIDE,
    )(*inputs)
    got = lax.all_to_all(sent, ("x", "c"), 0, 0, tiled=True).reshape(X * C * TOKENS, features)
    other = lax.ppermute(scaled, "c", [(0, 1), (1, 0)])
    counts_scratch = [
        pltpu.SMEM(slot_counts.shape, jnp.int32),
        pltpu.SemaphoreType.DMA((1,)),
    ]

    def shifted(array, by):
        pairs = [
            (c * Y + y, c * Y + (y + by * (1 - 2 * c)) % Y) for c in range(C) for y in range(Y)
        ]
        return lax.ppermute(array, ("c", "y"), pairs)

    def swapped(array, by):
        pairs = [(x * C + c, (x ^ by[c]) * C + c) for x in range(X) for c in range(C)]
        return lax.ppermute(array, ("x", "c"), pairs)

    def product(near, far, cots, total, last):
        begun = [] if total is None else [total]
        sums = shape((features, LANES), F32)
        total, laid = pl.pallas_call(
            lambda *refs: multiply_near(len(begun), *refs),
            out_shape=(sums, shape((Y, X, TOKENS, LANES), BF16)),
            in_specs=[VMEM] * 5 + [ANY] * 4 + [VMEM] * len(begun),
            out_specs=(VMEM, VMEM),
            scratch_shapes=[pltpu.SemaphoreType.DMA((X,))],
            compiler_params=PARAMS,
        )(*near, *cots, *begun)
        return pl.pallas_call(
            lambda *refs: multiply_far(zs, last, *refs),
            out_shape=shape((zs, BLK, COLS), F32) if last else sums,
            in_specs=[VMEM] * 5,
            out_specs=VMEM,
            compiler_params=PARAMS,
        )(*far, laid, total)

    total = None
    for wave in range(waves):
        unit, chip = pl.pallas_call(
            lambda *refs: compact(wave, *refs),
            out_shape=(
                shape((features, X * TOKENS), BF16),
                shape((Y * TOKENS, LANES), BF16),
            ),
            in_specs=[ANY, VMEM, VMEM, VMEM],
            out_specs=(VMEM, VMEM),
            scratch_shapes=counts_scratch,
            compiler_params=PARAMS,
        )(slot_counts, got, scaled, other)
        beside = [swapped(chip, by) for by in ((1, 3), (3, 1), (2, 2))]
        ahead, behind = shifted(unit, 2), shifted(unit, -2)
        near = [shifted(unit, 1), shifted(unit, -1)]
        far = [shifted(ahead, 1), shifted(behind, -1), shifted(ahead, 2)]
        cots = [c.reshape(-1, TOKENS, LANES) for c in (chip, *beside)]
        total = product([unit, *near, ahead, behind], far, cots, total, wave == waves - 1)
    return total.astype(F16)


def solution(mesh):
    split = Mesh(mesh.devices.reshape(-1, X, C, Y), ("z", "x", "c", "y"))
    dp = ("z", "x", "c")
    return jax.shard_map(
        body,
        mesh=split,
        in_specs=(P(dp, "y", None), P(dp, None, "y"), P(), P(dp), P(), P()),
        out_specs=P(dp, "y"),
        check_vma=False,
    )
```

```python
import jax
import jax.numpy as jnp
from jax import lax
from jax.experimental import pallas as pl
from jax.experimental.pallas import tpu as pltpu
from jax.sharding import Mesh, PartitionSpec as P

X, C, Y = 4, 2, 8
CAP = 12
ROWS = 40
PER = ROWS // Y
BLK = 40
COLS = 448
LANES = 512
TOKENS = 64
VIRTUAL = 576
RAISE = 64.0
F32, BF16, F16 = jnp.float32, jnp.bfloat16, jnp.float16
VMEM = pl.BlockSpec(memory_space=pltpu.VMEM)
SMEM = pl.BlockSpec(memory_space=pltpu.SMEM)
ANY = pl.BlockSpec(memory_space=pl.ANY)
PARAMS = pltpu.CompilerParams(vmem_limit_bytes=16 * 1024 * 1024)
WIDE = pltpu.CompilerParams(vmem_limit_bytes=56 * 1024 * 1024)


def iota(shape, axis):
    return lax.broadcasted_iota(jnp.int32, shape, axis)


def steps(value, width, most):
    return sum((value >= width * i).astype(jnp.int32) for i in range(1, most))


def fetch(pairs, sems):
    copies = [pltpu.make_async_copy(src, dst, sems.at[i]) for i, (src, dst) in enumerate(pairs)]
    for one in copies:
        one.start()
    return copies


def prepare(zs, *refs):
    sources, (out_ref, scaled_ref, fullest_ref), held = refs[:6], refs[6:9], refs[9:15]
    packed_ref, sems = refs[15:]
    act_ref, cot_ref, scales_ref, worker_ref, counts_ref, owned_ref = held
    copies = fetch(list(zip(sources, held)), sems)
    dp = (lax.axis_index("z") * X + lax.axis_index("x")) * C + lax.axis_index("c")
    slot = steps(iota((CAP * ROWS, 1), 0), ROWS, CAP)
    weight = jnp.zeros((CAP * ROWS, 1), F32)
    for one in copies[1:]:
        one.wait()
    count = counts_ref[dp]
    for s in range(CAP):
        looked_up = jnp.where(s < count, scales_ref[worker_ref[s]], 0.0)
        weight = jnp.where(slot == s, looked_up, weight)
    weight = weight / VIRTUAL
    scaled_ref[...] = (weight * cot_ref[...].astype(F32)).astype(BF16)

    def fuller(chip, most):
        return jnp.maximum(most, counts_ref[C * chip] + counts_ref[C * chip + 1])

    fullest_ref[0] = lax.fori_loop(0, counts_ref.shape[0] // C, fuller, 0)

    groups = -(-zs // 3)
    lane = iota((TOKENS, 128), 1)
    tiles = act_ref.shape[2] // 128
    copies[0].wait()

    def pack(tile, carry):
        at = pl.ds(pl.multiple_of(tile * 128, 128), 128)
        rows = [act_ref[t, :, at].astype(F32) for t in range(PER)]
        rows.append(jnp.zeros((TOKENS - PER * CAP, 128), F32))
        packed_ref[:, at] = jnp.concatenate(rows, 0)
        return carry

    lax.fori_loop(0, tiles, pack, 0)

    def feature_block(f, carry):
        for g in range(groups):
            full = jnp.zeros((TOKENS, 128), F32)
            for j in range(min(3, zs - 3 * g)):
                start = owned_ref[(3 * g + j) * X * C + f] * BLK
                tile = jnp.minimum(start // 128, tiles - 2)
                shift = lax.rem(BLK * j - (start - tile * 128) + 256, 256)
                window = pl.ds(pl.multiple_of(tile * 128, 128), 256)
                rolled = pltpu.roll(packed_ref[:, window], shift, 1)[:, :128]
                full = jnp.where((lane >= BLK * j) & (lane < BLK * (j + 1)), rolled, full)
            out_ref[f, :, 128 * g : 128 * (g + 1)] = full.astype(BF16)
        return carry

    lax.fori_loop(0, X * C, feature_block, 0)


def pick(codes_out, codes_in):
    return jnp.where(codes_out == codes_in, 1.0, 0.0).astype(BF16)


def compact(wave, counts_hbm, got_ref, own_ref, other_ref, unit_ref, chip_ref, counts_ref, sems):
    copies = fetch([(counts_hbm, counts_ref)], sems)
    compact_act(wave, copies, counts_ref, got_ref, unit_ref)
    compact_cot(wave, counts_ref, own_ref, other_ref, chip_ref)


def compact_act(wave, copies, counts_ref, got_ref, out_ref):
    base = lax.axis_index("z") * X * C
    m = iota((2 * TOKENS, 1), 0)
    half = (m >= TOKENS).astype(jnp.int32)
    row = m - TOKENS * half
    t = steps(row, CAP, 6)
    code_out = jnp.where(row < PER * CAP, half * 10000 + t * 100 + row - CAP * t, -2)
    k = iota((1, 2 * C * TOKENS), 1)
    block = steps(k, TOKENS, 2 * C)
    row = k - TOKENS * block
    t = steps(row, CAP, 6)
    s = row - CAP * t
    half = block >> 1
    core = block & 1
    for one in copies:
        one.wait()
    for p in range(X // 2):
        n = [counts_ref[base + 4 * p + i] for i in range(4)]
        live = jnp.where(
            half == 1, jnp.where(core == 1, n[3], n[2]), jnp.where(core == 1, n[1], n[0])
        )
        place = s + core * jnp.where(half == 1, n[2], n[0]) - CAP * wave
        there = (row < PER * CAP) & (s < live) & (place >= 0) & (place < CAP)
        code_in = jnp.where(there, half * 10000 + t * 100 + place, -1)
        got = got_ref[2 * C * p * TOKENS : 2 * C * (p + 1) * TOKENS, :]
        out = lax.dot_general(
            got, pick(code_out, code_in), (((0,), (1,)), ((), ())), preferred_element_type=F32
        )
        out_ref[:, 128 * p : 128 * (p + 1)] = out.astype(BF16)


def compact_cot(wave, counts_ref, own_ref, other_ref, out_ref):
    base = (lax.axis_index("z") * X + lax.axis_index("x")) * C
    me = lax.axis_index("c")
    first = counts_ref[base]
    k = iota((1, CAP * ROWS), 1)
    slot = steps(k, ROWS, CAP)
    row_in = k - ROWS * slot
    codes = []
    for core in (me, 1 - me):
        place = slot + core * first - CAP * wave
        there = (slot < counts_ref[base + core]) & (place >= 0) & (place < CAP)
        codes.append(jnp.where(there, row_in * 100 + place, -1))
    m = iota((2 * TOKENS, 1), 0)
    half = (m >= TOKENS).astype(jnp.int32)
    row = m - TOKENS * half
    t = steps(row, CAP, 6)
    for p in range(Y // 2):
        r = PER * (2 * p + half) + t
        code_out = jnp.where(row < PER * CAP, r * 100 + row - CAP * t, -2)
        out = jnp.dot(pick(code_out, codes[0]), own_ref[...], preferred_element_type=F32)
        out += jnp.dot(pick(code_out, codes[1]), other_ref[...], preferred_element_type=F32)
        full = jnp.concatenate([out, jnp.zeros((2 * TOKENS, LANES - COLS), F32)], 1)
        out_ref[2 * TOKENS * p : 2 * TOKENS * (p + 1), :] = full.astype(BF16)


def multiply_near(begun, *refs):
    acts, cots, rest = refs[:5], refs[5:9], refs[9 + begun :]
    out_ref, cot_ref, sems = rest
    x, y, c = lax.axis_index("x"), lax.axis_index("y"), lax.axis_index("c")
    near = 1 + 2 * c
    places = [
        (ref, cot_ref.at[:, x ^ by]) for ref, by in zip(cots, (0, near, 4 - near, 2))
    ]
    for copy in fetch(places, sems):
        copy.wait()
    total = refs[9][...] if begun else jnp.zeros(out_ref.shape, F32)
    out_ref[...] = total + outer(y, c, acts, (0, 1, -1, 2, -2), cot_ref)


def outer(y, c, acts, ks, cot_ref):
    total = jnp.zeros((acts[0].shape[0], LANES), F32)
    for k, ref in zip(ks, acts):
        cot = cot_ref[lax.rem(y - (1 - 2 * c) * k + Y, Y)].reshape(X * TOKENS, LANES)
        total += jnp.dot(ref[...], cot, preferred_element_type=F32)
    return total


def multiply_far(zs, last, *refs):
    acts, (cot_ref, total_ref, out_ref) = refs[:3], refs[3:]
    y, c = lax.axis_index("y"), lax.axis_index("c")
    total = total_ref[...] + outer(y, c, acts, (3, -3, 4), cot_ref)
    if not last:
        out_ref[...] = total
        return
    for z in range(zs):
        begin = 128 * (z // 3) + BLK * (z % 3)
        out_ref[z] = total[begin : begin + BLK, :COLS] * RAISE


def body(*inputs):
    term, fullest = partial_sums(*inputs)
    term = lax.cond(
        fullest > CAP, lambda done, *again: partial_sums(*again, waves=C)[0], lambda done, *_: done,
        term, *inputs,
    )
    parts = lax.all_to_all(term, "z", 0, 0, tiled=True)
    return jnp.sum(parts.astype(F32) * (1.0 / RAISE), axis=0)


def partial_sums(
    activations, cotangent, scales, slot_worker, slot_counts, owned_block, waves=1
):
    zs = lax.axis_size("z")
    features = 128 * (-(-zs // 3))
    shape = jax.ShapeDtypeStruct
    act = jnp.transpose(activations, (1, 0, 2))
    cot = cotangent.reshape(CAP * ROWS, COLS)
    inputs = (act, cot, scales, slot_worker, slot_counts, owned_block)
    sent, scaled, fullest = pl.pallas_call(
        lambda *refs: prepare(zs, *refs),
        out_shape=(
            pltpu.VMEM((X * C, TOKENS, features), BF16),
            pltpu.VMEM(cot.shape, BF16),
            shape((1,), jnp.int32),
        ),
        in_specs=[ANY] * 6,
        out_specs=(VMEM, VMEM, SMEM),
        scratch_shapes=[
            *[pltpu.VMEM(a.shape, a.dtype) for a in inputs[:2]],
            *[pltpu.SMEM(a.shape, a.dtype) for a in inputs[2:]],
            pltpu.VMEM((TOKENS, act.shape[2]), F32),
            pltpu.SemaphoreType.DMA((6,)),
        ],
        compiler_params=WIDE,
    )(*inputs)
    got = lax.all_to_all(sent, ("x", "c"), 0, 0, tiled=True).reshape(X * C * TOKENS, features)
    other = lax.ppermute(scaled, "c", [(0, 1), (1, 0)])
    counts_scratch = [
        pltpu.SMEM(slot_counts.shape, jnp.int32),
        pltpu.SemaphoreType.DMA((1,)),
    ]

    def shifted(array, by):
        pairs = [
            (c * Y + y, c * Y + (y + by * (1 - 2 * c)) % Y) for c in range(C) for y in range(Y)
        ]
        return lax.ppermute(array, ("c", "y"), pairs)

    def swapped(array, by):
        pairs = [(x * C + c, (x ^ by[c]) * C + c) for x in range(X) for c in range(C)]
        return lax.ppermute(array, ("x", "c"), pairs)

    def product(near, far, cots, total, last):
        begun = [] if total is None else [total]
        sums = shape((features, LANES), F32)
        total, laid = pl.pallas_call(
            lambda *refs: multiply_near(len(begun), *refs),
            out_shape=(sums, shape((Y, X, TOKENS, LANES), BF16)),
            in_specs=[VMEM] * 5 + [ANY] * 4 + [VMEM] * len(begun),
            out_specs=(VMEM, VMEM),
            scratch_shapes=[pltpu.SemaphoreType.DMA((X,))],
            compiler_params=PARAMS,
        )(*near, *cots, *begun)
        return pl.pallas_call(
            lambda *refs: multiply_far(zs, last, *refs),
            out_shape=shape((zs, BLK, COLS), F32) if last else sums,
            in_specs=[VMEM] * 5,
            out_specs=VMEM,
            compiler_params=PARAMS,
        )(*far, laid, total)

    total = None
    for wave in range(waves):
        unit, chip = pl.pallas_call(
            lambda *refs: compact(wave, *refs),
            out_shape=(
                shape((features, X * TOKENS), BF16),
                shape((Y * TOKENS, LANES), BF16),
            ),
            in_specs=[ANY, VMEM, VMEM, VMEM],
            out_specs=(VMEM, VMEM),
            scratch_shapes=counts_scratch,
            compiler_params=PARAMS,
        )(slot_counts, got, scaled, other)
        beside = [swapped(chip, by) for by in ((1, 3), (3, 1), (2, 2))]
        ahead, behind = shifted(unit, 2), shifted(unit, -2)
        near = [shifted(unit, 1), shifted(unit, -1)]
        far = [shifted(ahead, 1), shifted(behind, -1), shifted(ahead, 2)]
        cots = [c.reshape(-1, TOKENS, LANES) for c in (chip, *beside)]
        total = product([unit, *near, ahead, behind], far, cots, total, wave == waves - 1)
    return total.astype(F16), fullest[0]


def solution(mesh):
    split = Mesh(mesh.devices.reshape(-1, X, C, Y), ("z", "x", "c", "y"))
    dp = ("z", "x", "c")
    return jax.shard_map(
        body,
        mesh=split,
        in_specs=(P(dp, "y", None), P(dp, None, "y"), P(), P(dp), P(), P()),
        out_specs=P(dp, "y"),
        check_vma=False,
    )
```

```python
import jax
import jax.numpy as jnp
from jax import lax
from jax.experimental import pallas as pl
from jax.experimental.pallas import tpu as pltpu
from jax.sharding import Mesh, PartitionSpec as P

X, C, Y = 4, 2, 8
CAP = 12
ROWS = 40
PER = ROWS // Y
BLK = 40
COLS = 448
LANES = 512
TOKENS = 64
VIRTUAL = 576
RAISE = 64.0
F32, BF16, F16 = jnp.float32, jnp.bfloat16, jnp.float16
VMEM = pl.BlockSpec(memory_space=pltpu.VMEM)
SMEM = pl.BlockSpec(memory_space=pltpu.SMEM)
ANY = pl.BlockSpec(memory_space=pl.ANY)
PARAMS = pltpu.CompilerParams(vmem_limit_bytes=16 * 1024 * 1024)
WIDE = pltpu.CompilerParams(vmem_limit_bytes=56 * 1024 * 1024)


def iota(shape, axis):
    return lax.broadcasted_iota(jnp.int32, shape, axis)


def steps(value, width, most):
    return sum((value >= width * i).astype(jnp.int32) for i in range(1, most))


def fetch(pairs, sems):
    copies = [pltpu.make_async_copy(src, dst, sems.at[i]) for i, (src, dst) in enumerate(pairs)]
    for one in copies:
        one.start()
    return copies


def prepare(zs, *refs):
    sources, (out_ref, scaled_ref, fullest_ref), held = refs[:6], refs[6:9], refs[9:15]
    sems = refs[15]
    act_ref, cot_ref, scales_ref, worker_ref, counts_ref, owned_ref = held
    copies = fetch(list(zip(sources, held)), sems)
    dp = (lax.axis_index("z") * X + lax.axis_index("x")) * C + lax.axis_index("c")
    slot = steps(iota((CAP * ROWS, 1), 0), ROWS, CAP)
    weight = jnp.zeros((CAP * ROWS, 1), F32)
    for one in copies[1:]:
        one.wait()
    count = counts_ref[dp]
    for s in range(CAP):
        looked_up = jnp.where(s < count, scales_ref[worker_ref[s]], 0.0)
        weight = jnp.where(slot == s, looked_up, weight)
    weight = weight / VIRTUAL
    scaled_ref[...] = (weight * cot_ref[...].astype(F32)).astype(BF16)

    def fuller(chip, most):
        return jnp.maximum(most, counts_ref[C * chip] + counts_ref[C * chip + 1])

    fullest_ref[0] = lax.fori_loop(0, counts_ref.shape[0] // C, fuller, 0)

    groups = -(-zs // 3)
    lane = iota((CAP, 128), 1)
    last = act_ref.shape[2] // 128 - 2
    copies[0].wait()

    def feature_block(f, carry):
        for g in range(groups):
            tiles = [jnp.zeros((CAP, 128), F32) for _ in range(PER)]
            for j in range(min(3, zs - 3 * g)):
                start = owned_ref[(3 * g + j) * X * C + f] * BLK
                tile = jnp.minimum(start // 128, last)
                shift = lax.rem(BLK * j - (start - tile * 128) + 256, 256)
                window = pl.ds(pl.multiple_of(tile * 128, 128), 256)
                keep = (lane >= BLK * j) & (lane < BLK * (j + 1))
                for t in range(PER):
                    rolled = pltpu.roll(act_ref[t, :, window].astype(F32), shift, 1)
                    tiles[t] = jnp.where(keep, rolled[:, :128], tiles[t])
            full = jnp.concatenate([*tiles, jnp.zeros((TOKENS - PER * CAP, 128), F32)], 0)
            out_ref[f, :, 128 * g : 128 * (g + 1)] = full.astype(BF16)
        return carry

    lax.fori_loop(0, X * C, feature_block, 0)


def pick(codes_out, codes_in):
    return jnp.where(codes_out == codes_in, 1.0, 0.0).astype(BF16)


def compact(wave, counts_hbm, got_ref, own_ref, other_ref, unit_ref, chip_ref, counts_ref, sems):
    copies = fetch([(counts_hbm, counts_ref)], sems)
    compact_act(wave, copies, counts_ref, got_ref, unit_ref)
    compact_cot(wave, counts_ref, own_ref, other_ref, chip_ref)


def compact_act(wave, copies, counts_ref, got_ref, out_ref):
    base = lax.axis_index("z") * X * C
    m = iota((2 * TOKENS, 1), 0)
    half = (m >= TOKENS).astype(jnp.int32)
    row = m - TOKENS * half
    t = steps(row, CAP, 6)
    code_out = jnp.where(row < PER * CAP, half * 10000 + t * 100 + row - CAP * t, -2)
    k = iota((1, 2 * C * TOKENS), 1)
    block = steps(k, TOKENS, 2 * C)
    row = k - TOKENS * block
    t = steps(row, CAP, 6)
    s = row - CAP * t
    half = block >> 1
    core = block & 1
    for one in copies:
        one.wait()
    for p in range(X // 2):
        n = [counts_ref[base + 4 * p + i] for i in range(4)]
        live = jnp.where(
            half == 1, jnp.where(core == 1, n[3], n[2]), jnp.where(core == 1, n[1], n[0])
        )
        place = s + core * jnp.where(half == 1, n[2], n[0]) - CAP * wave
        there = (row < PER * CAP) & (s < live) & (place >= 0) & (place < CAP)
        code_in = jnp.where(there, half * 10000 + t * 100 + place, -1)
        got = got_ref[2 * C * p * TOKENS : 2 * C * (p + 1) * TOKENS, :]
        out = lax.dot_general(
            got, pick(code_out, code_in), (((0,), (1,)), ((), ())), preferred_element_type=F32
        )
        out_ref[:, 128 * p : 128 * (p + 1)] = out.astype(BF16)


def compact_cot(wave, counts_ref, own_ref, other_ref, out_ref):
    base = (lax.axis_index("z") * X + lax.axis_index("x")) * C
    me = lax.axis_index("c")
    first = counts_ref[base]
    k = iota((1, CAP * ROWS), 1)
    slot = steps(k, ROWS, CAP)
    row_in = k - ROWS * slot
    codes = []
    for core in (me, 1 - me):
        place = slot + core * first - CAP * wave
        there = (slot < counts_ref[base + core]) & (place >= 0) & (place < CAP)
        codes.append(jnp.where(there, row_in * 100 + place, -1))
    m = iota((2 * TOKENS, 1), 0)
    half = (m >= TOKENS).astype(jnp.int32)
    row = m - TOKENS * half
    t = steps(row, CAP, 6)
    for p in range(Y // 2):
        r = PER * (2 * p + half) + t
        code_out = jnp.where(row < PER * CAP, r * 100 + row - CAP * t, -2)
        out = jnp.dot(pick(code_out, codes[0]), own_ref[...], preferred_element_type=F32)
        out += jnp.dot(pick(code_out, codes[1]), other_ref[...], preferred_element_type=F32)
        full = jnp.concatenate([out, jnp.zeros((2 * TOKENS, LANES - COLS), F32)], 1)
        out_ref[2 * TOKENS * p : 2 * TOKENS * (p + 1), :] = full.astype(BF16)


def join(after_ref, one_ref, two_ref, out_ref, sems):
    rows = one_ref.shape[0]
    halves = [(one_ref, out_ref.at[0:rows]), (two_ref, out_ref.at[rows : 2 * rows])]
    for copy in fetch(halves, sems):
        copy.wait()


def multiply_near(begun, *refs):
    acts, (own, one, pair), rest = refs[:5], refs[5:8], refs[8 + begun :]
    out_ref, cot_ref, sems = rest
    x, y, c = lax.axis_index("x"), lax.axis_index("y"), lax.axis_index("c")
    near = 1 + 2 * c
    places = [
        (own, cot_ref.at[:, x]),
        (one, cot_ref.at[:, x ^ near]),
        (pair.at[0:Y], cot_ref.at[:, x ^ (4 - near)]),
        (pair.at[Y : 2 * Y], cot_ref.at[:, x ^ 2]),
    ]
    for copy in fetch(places, sems):
        copy.wait()
    total = refs[8][...] if begun else jnp.zeros(out_ref.shape, F32)
    out_ref[...] = total + outer(y, c, acts, (0, 1, -1, 2, -2), cot_ref)


def outer(y, c, acts, ks, cot_ref):
    total = jnp.zeros((acts[0].shape[0], LANES), F32)
    for k, ref in zip(ks, acts):
        cot = cot_ref[lax.rem(y - (1 - 2 * c) * k + Y, Y)].reshape(X * TOKENS, LANES)
        total += jnp.dot(ref[...], cot, preferred_element_type=F32)
    return total


def multiply_far(zs, last, *refs):
    acts, (cot_ref, total_ref, out_ref) = refs[:3], refs[3:]
    y, c = lax.axis_index("y"), lax.axis_index("c")
    total = total_ref[...] + outer(y, c, acts, (3, -3, 4), cot_ref)
    if not last:
        out_ref[...] = total
        return
    for z in range(zs):
        begin = 128 * (z // 3) + BLK * (z % 3)
        out_ref[z] = total[begin : begin + BLK, :COLS] * RAISE


def body(*inputs):
    term, fullest = partial_sums(*inputs)
    term = lax.cond(
        fullest > CAP, lambda done, *again: partial_sums(*again, waves=C)[0], lambda done, *_: done,
        term, *inputs,
    )
    parts = lax.all_to_all(term, "z", 0, 0, tiled=True)
    return jnp.sum(parts.astype(F32) * (1.0 / RAISE), axis=0)


def partial_sums(
    activations, cotangent, scales, slot_worker, slot_counts, owned_block, waves=1
):
    zs = lax.axis_size("z")
    features = 128 * (-(-zs // 3))
    shape = jax.ShapeDtypeStruct
    act = jnp.transpose(activations, (1, 0, 2))
    cot = cotangent.reshape(CAP * ROWS, COLS)
    inputs = (act, cot, scales, slot_worker, slot_counts, owned_block)
    sent, scaled, fullest = pl.pallas_call(
        lambda *refs: prepare(zs, *refs),
        out_shape=(
            pltpu.VMEM((X * C, TOKENS, features), BF16),
            pltpu.VMEM(cot.shape, BF16),
            shape((1,), jnp.int32),
        ),
        in_specs=[ANY] * 6,
        out_specs=(VMEM, VMEM, SMEM),
        scratch_shapes=[
            *[pltpu.VMEM(a.shape, a.dtype) for a in inputs[:2]],
            *[pltpu.SMEM(a.shape, a.dtype) for a in inputs[2:]],
            pltpu.SemaphoreType.DMA((6,)),
        ],
        compiler_params=WIDE,
    )(*inputs)
    got = lax.all_to_all(sent, ("x", "c"), 0, 0, tiled=True).reshape(X * C * TOKENS, features)
    other = lax.ppermute(scaled, "c", [(0, 1), (1, 0)])
    counts_scratch = [
        pltpu.SMEM(slot_counts.shape, jnp.int32),
        pltpu.SemaphoreType.DMA((1,)),
    ]

    def shifted(array, by):
        pairs = [
            (c * Y + y, c * Y + (y + by * (1 - 2 * c)) % Y) for c in range(C) for y in range(Y)
        ]
        return lax.ppermute(array, ("c", "y"), pairs)

    def swapped(array, by):
        pairs = [(x * C + c, (x ^ by[c]) * C + c) for x in range(X) for c in range(C)]
        return lax.ppermute(array, ("x", "c"), pairs)

    def product(near, far, cots, total, last):
        begun = [] if total is None else [total]
        sums = shape((features, LANES), F32)
        total, laid = pl.pallas_call(
            lambda *refs: multiply_near(len(begun), *refs),
            out_shape=(sums, shape((Y, X, TOKENS, LANES), BF16)),
            in_specs=[VMEM] * 5 + [ANY] * 3 + [VMEM] * len(begun),
            out_specs=(VMEM, VMEM),
            scratch_shapes=[pltpu.SemaphoreType.DMA((X,))],
            compiler_params=PARAMS,
        )(*near, *cots, *begun)
        return pl.pallas_call(
            lambda *refs: multiply_far(zs, last, *refs),
            out_shape=shape((zs, BLK, COLS), F32) if last else sums,
            in_specs=[VMEM] * 5,
            out_specs=VMEM,
            compiler_params=PARAMS,
        )(*far, laid, total)

    total = None
    for wave in range(waves):
        unit, chip = pl.pallas_call(
            lambda *refs: compact(wave, *refs),
            out_shape=(
                shape((features, X * TOKENS), BF16),
                shape((Y * TOKENS, LANES), BF16),
            ),
            in_specs=[ANY, VMEM, VMEM, VMEM],
            out_specs=(VMEM, VMEM),
            scratch_shapes=counts_scratch,
            compiler_params=PARAMS,
        )(slot_counts, got, scaled, other)
        one = swapped(chip, (1, 3))
        ahead, behind = shifted(unit, 2), shifted(unit, -2)
        near = [shifted(unit, 1), shifted(unit, -1)]
        far = [shifted(ahead, 1), shifted(behind, -1), shifted(ahead, 2)]
        both = pl.pallas_call(
            join,
            out_shape=shape((2 * chip.shape[0], LANES), BF16),
            in_specs=[ANY, ANY, ANY],
            out_specs=ANY,
            scratch_shapes=[pltpu.SemaphoreType.DMA((2,))],
            compiler_params=PARAMS,
        )(ahead, chip, one)
        pair = swapped(both, (3, 1))
        cots = [c.reshape(-1, TOKENS, LANES) for c in (chip, one, pair)]
        total = product([unit, *near, ahead, behind], far, cots, total, wave == waves - 1)
    return total.astype(F16), fullest[0]


def solution(mesh):
    split = Mesh(mesh.devices.reshape(-1, X, C, Y), ("z", "x", "c", "y"))
    dp = ("z", "x", "c")
    return jax.shard_map(
        body,
        mesh=split,
        in_specs=(P(dp, "y", None), P(dp, None, "y"), P(), P(dp), P(), P()),
        out_specs=P(dp, "y"),
        check_vma=False,
    )
```

```python
import jax
import jax.numpy as jnp
from jax import lax
from jax.experimental import pallas as pl
from jax.experimental.pallas import tpu as pltpu
from jax.sharding import Mesh, PartitionSpec as P

X, C, Y = 4, 2, 8
CAP = 12
ROWS = 40
PER = ROWS // Y
BLK = 40
COLS = 448
LANES = 512
TOKENS = 64
VIRTUAL = 576
RAISE = 64.0
F32, BF16, F16 = jnp.float32, jnp.bfloat16, jnp.float16
VMEM = pl.BlockSpec(memory_space=pltpu.VMEM)
SMEM = pl.BlockSpec(memory_space=pltpu.SMEM)
ANY = pl.BlockSpec(memory_space=pl.ANY)
PARAMS = pltpu.CompilerParams(vmem_limit_bytes=16 * 1024 * 1024)
WIDE = pltpu.CompilerParams(vmem_limit_bytes=56 * 1024 * 1024)


def iota(shape, axis):
    return lax.broadcasted_iota(jnp.int32, shape, axis)


def steps(value, width, most):
    return sum((value >= width * i).astype(jnp.int32) for i in range(1, most))


def fetch(pairs, sems):
    copies = [pltpu.make_async_copy(src, dst, sems.at[i]) for i, (src, dst) in enumerate(pairs)]
    for one in copies:
        one.start()
    return copies


def prepare(zs, *refs):
    sources, (out_ref, scaled_ref, fullest_ref), held = refs[:6], refs[6:9], refs[9:15]
    sems = refs[15]
    act_ref, cot_ref, scales_ref, worker_ref, counts_ref, owned_ref = held
    copies = fetch(list(zip(sources, held)), sems)
    dp = (lax.axis_index("z") * X + lax.axis_index("x")) * C + lax.axis_index("c")
    slot = steps(iota((CAP * ROWS, 1), 0), ROWS, CAP)
    weight = jnp.zeros((CAP * ROWS, 1), F32)
    for one in copies[1:]:
        one.wait()
    count = counts_ref[dp]
    for s in range(CAP):
        looked_up = jnp.where(s < count, scales_ref[worker_ref[s]], 0.0)
        weight = jnp.where(slot == s, looked_up, weight)
    weight = weight / VIRTUAL
    scaled_ref[...] = (weight * cot_ref[...].astype(F32)).astype(BF16)

    def fuller(chip, most):
        return jnp.maximum(most, counts_ref[C * chip] + counts_ref[C * chip + 1])

    fullest_ref[0] = lax.fori_loop(0, counts_ref.shape[0] // C, fuller, 0)

    groups = -(-zs // 3)
    lane = iota((CAP, 128), 1)
    last = act_ref.shape[2] // 128 - 2
    copies[0].wait()

    def feature_block(f, carry):
        for g in range(groups):
            tiles = [jnp.zeros((CAP, 128), F32) for _ in range(PER)]
            for j in range(min(3, zs - 3 * g)):
                start = owned_ref[(3 * g + j) * X * C + f] * BLK
                tile = jnp.minimum(start // 128, last)
                shift = lax.rem(BLK * j - (start - tile * 128) + 256, 256)
                window = pl.ds(pl.multiple_of(tile * 128, 128), 256)
                keep = (lane >= BLK * j) & (lane < BLK * (j + 1))
                for t in range(PER):
                    rolled = pltpu.roll(act_ref[t, :, window].astype(F32), shift, 1)
                    tiles[t] = jnp.where(keep, rolled[:, :128], tiles[t])
            full = jnp.concatenate([*tiles, jnp.zeros((TOKENS - PER * CAP, 128), F32)], 0)
            out_ref[f, :, 128 * g : 128 * (g + 1)] = full.astype(BF16)
        return carry

    lax.fori_loop(0, X * C, feature_block, 0)


def pick(codes_out, codes_in):
    return jnp.where(codes_out == codes_in, 1.0, 0.0).astype(BF16)


def compact_act(wave, counts_hbm, got_ref, out_ref, counts_ref, sems):
    copies = fetch([(counts_hbm, counts_ref)], sems)
    base = lax.axis_index("z") * X * C
    m = iota((2 * TOKENS, 1), 0)
    half = (m >= TOKENS).astype(jnp.int32)
    row = m - TOKENS * half
    t = steps(row, CAP, 6)
    code_out = jnp.where(row < PER * CAP, half * 10000 + t * 100 + row - CAP * t, -2)
    k = iota((1, 2 * C * TOKENS), 1)
    block = steps(k, TOKENS, 2 * C)
    row = k - TOKENS * block
    t = steps(row, CAP, 6)
    s = row - CAP * t
    half = block >> 1
    core = block & 1
    for one in copies:
        one.wait()
    for p in range(X // 2):
        n = [counts_ref[base + 4 * p + i] for i in range(4)]
        live = jnp.where(
            half == 1, jnp.where(core == 1, n[3], n[2]), jnp.where(core == 1, n[1], n[0])
        )
        place = s + core * jnp.where(half == 1, n[2], n[0]) - CAP * wave
        there = (row < PER * CAP) & (s < live) & (place >= 0) & (place < CAP)
        code_in = jnp.where(there, half * 10000 + t * 100 + place, -1)
        got = got_ref[2 * C * p * TOKENS : 2 * C * (p + 1) * TOKENS, :]
        out = lax.dot_general(
            got, pick(code_out, code_in), (((0,), (1,)), ((), ())), preferred_element_type=F32
        )
        out_ref[:, 128 * p : 128 * (p + 1)] = out.astype(BF16)


def compact_cot(wave, counts_hbm, own_ref, other_ref, out_ref, counts_ref, sems):
    copies = fetch([(counts_hbm, counts_ref)], sems)
    base = (lax.axis_index("z") * X + lax.axis_index("x")) * C
    me = lax.axis_index("c")
    for one in copies:
        one.wait()
    first = counts_ref[base]
    k = iota((1, CAP * ROWS), 1)
    slot = steps(k, ROWS, CAP)
    row_in = k - ROWS * slot
    codes = []
    for core in (me, 1 - me):
        place = slot + core * first - CAP * wave
        there = (slot < counts_ref[base + core]) & (place >= 0) & (place < CAP)
        codes.append(jnp.where(there, row_in * 100 + place, -1))
    m = iota((2 * TOKENS, 1), 0)
    half = (m >= TOKENS).astype(jnp.int32)
    row = m - TOKENS * half
    t = steps(row, CAP, 6)
    for p in range(Y // 2):
        r = PER * (2 * p + half) + t
        code_out = jnp.where(row < PER * CAP, r * 100 + row - CAP * t, -2)
        out = jnp.dot(pick(code_out, codes[0]), own_ref[...], preferred_element_type=F32)
        out += jnp.dot(pick(code_out, codes[1]), other_ref[...], preferred_element_type=F32)
        full = jnp.concatenate([out, jnp.zeros((2 * TOKENS, LANES - COLS), F32)], 1)
        out_ref[2 * TOKENS * p : 2 * TOKENS * (p + 1), :] = full.astype(BF16)


def join(after_ref, one_ref, two_ref, out_ref, sems):
    rows = one_ref.shape[0]
    halves = [(one_ref, out_ref.at[0:rows]), (two_ref, out_ref.at[rows : 2 * rows])]
    for copy in fetch(halves, sems):
        copy.wait()


def multiply_near(begun, *refs):
    acts, (own, one, pair), rest = refs[:5], refs[5:8], refs[8 + begun :]
    out_ref, cot_ref, sems = rest
    x, y, c = lax.axis_index("x"), lax.axis_index("y"), lax.axis_index("c")
    near = 1 + 2 * c
    places = [
        (own, cot_ref.at[:, x]),
        (one, cot_ref.at[:, x ^ near]),
        (pair.at[0:Y], cot_ref.at[:, x ^ (4 - near)]),
        (pair.at[Y : 2 * Y], cot_ref.at[:, x ^ 2]),
    ]
    for copy in fetch(places, sems):
        copy.wait()
    total = refs[8][...] if begun else jnp.zeros(out_ref.shape, F32)
    out_ref[...] = total + outer(y, c, acts, (0, 1, -1, 2, -2), cot_ref)


def outer(y, c, acts, ks, cot_ref):
    total = jnp.zeros((acts[0].shape[0], LANES), F32)
    for k, ref in zip(ks, acts):
        cot = cot_ref[lax.rem(y - (1 - 2 * c) * k + Y, Y)].reshape(X * TOKENS, LANES)
        total += jnp.dot(ref[...], cot, preferred_element_type=F32)
    return total


def multiply_far(zs, last, *refs):
    acts, (cot_ref, total_ref, out_ref) = refs[:3], refs[3:]
    y, c = lax.axis_index("y"), lax.axis_index("c")
    total = total_ref[...] + outer(y, c, acts, (3, -3, 4), cot_ref)
    if not last:
        out_ref[...] = total
        return
    for z in range(zs):
        begin = 128 * (z // 3) + BLK * (z % 3)
        out_ref[z] = total[begin : begin + BLK, :COLS] * RAISE


def body(*inputs):
    term, fullest = partial_sums(*inputs)
    term = lax.cond(
        fullest > CAP, lambda done, *again: partial_sums(*again, waves=C)[0], lambda done, *_: done,
        term, *inputs,
    )
    parts = lax.all_to_all(term, "z", 0, 0, tiled=True)
    return jnp.sum(parts.astype(F32) * (1.0 / RAISE), axis=0)


def partial_sums(
    activations, cotangent, scales, slot_worker, slot_counts, owned_block, waves=1
):
    zs = lax.axis_size("z")
    features = 128 * (-(-zs // 3))
    shape = jax.ShapeDtypeStruct
    act = jnp.transpose(activations, (1, 0, 2))
    cot = cotangent.reshape(CAP * ROWS, COLS)
    inputs = (act, cot, scales, slot_worker, slot_counts, owned_block)
    sent, scaled, fullest = pl.pallas_call(
        lambda *refs: prepare(zs, *refs),
        out_shape=(
            pltpu.VMEM((X * C, TOKENS, features), BF16),
            pltpu.VMEM(cot.shape, BF16),
            shape((1,), jnp.int32),
        ),
        in_specs=[ANY] * 6,
        out_specs=(VMEM, VMEM, SMEM),
        scratch_shapes=[
            *[pltpu.VMEM(a.shape, a.dtype) for a in inputs[:2]],
            *[pltpu.SMEM(a.shape, a.dtype) for a in inputs[2:]],
            pltpu.SemaphoreType.DMA((6,)),
        ],
        compiler_params=WIDE,
    )(*inputs)
    got = lax.all_to_all(sent, ("x", "c"), 0, 0, tiled=True).reshape(X * C * TOKENS, features)
    other = lax.ppermute(scaled, "c", [(0, 1), (1, 0)])
    counts_scratch = [
        pltpu.SMEM(slot_counts.shape, jnp.int32),
        pltpu.SemaphoreType.DMA((1,)),
    ]

    def shifted(array, by):
        pairs = [
            (c * Y + y, c * Y + (y + by * (1 - 2 * c)) % Y) for c in range(C) for y in range(Y)
        ]
        return lax.ppermute(array, ("c", "y"), pairs)

    def swapped(array, by):
        pairs = [(x * C + c, (x ^ by[c]) * C + c) for x in range(X) for c in range(C)]
        return lax.ppermute(array, ("x", "c"), pairs)

    def product(near, far, cots, total, last):
        begun = [] if total is None else [total]
        sums = shape((features, LANES), F32)
        total, laid = pl.pallas_call(
            lambda *refs: multiply_near(len(begun), *refs),
            out_shape=(sums, shape((Y, X, TOKENS, LANES), BF16)),
            in_specs=[VMEM] * 5 + [ANY] * 3 + [VMEM] * len(begun),
            out_specs=(VMEM, VMEM),
            scratch_shapes=[pltpu.SemaphoreType.DMA((X,))],
            compiler_params=PARAMS,
        )(*near, *cots, *begun)
        return pl.pallas_call(
            lambda *refs: multiply_far(zs, last, *refs),
            out_shape=shape((zs, BLK, COLS), F32) if last else sums,
            in_specs=[VMEM] * 5,
            out_specs=VMEM,
            compiler_params=PARAMS,
        )(*far, laid, total)

    total = None
    for wave in range(waves):
        unit = pl.pallas_call(
            lambda *refs: compact_act(wave, *refs),
            out_shape=shape((features, X * TOKENS), BF16),
            in_specs=[ANY, VMEM],
            out_specs=VMEM,
            scratch_shapes=counts_scratch,
            compiler_params=PARAMS,
        )(slot_counts, got)
        chip = pl.pallas_call(
            lambda *refs: compact_cot(wave, *refs),
            out_shape=shape((Y * TOKENS, LANES), BF16),
            in_specs=[ANY, VMEM, VMEM],
            out_specs=VMEM,
            scratch_shapes=counts_scratch,
            compiler_params=PARAMS,
        )(slot_counts, scaled, other)
        one = swapped(chip, (1, 3))
        ahead, behind = shifted(unit, 2), shifted(unit, -2)
        near = [shifted(unit, 1), shifted(unit, -1)]
        far = [shifted(ahead, 1), shifted(behind, -1), shifted(ahead, 2)]
        both = pl.pallas_call(
            join,
            out_shape=shape((2 * chip.shape[0], LANES), BF16),
            in_specs=[ANY, ANY, ANY],
            out_specs=ANY,
            scratch_shapes=[pltpu.SemaphoreType.DMA((2,))],
            compiler_params=PARAMS,
        )(near[0], chip, one)
        pair = swapped(both, (3, 1))
        cots = [c.reshape(-1, TOKENS, LANES) for c in (chip, one, pair)]
        total = product([unit, *near, ahead, behind], far, cots, total, wave == waves - 1)
    return total.astype(F16), fullest[0]


def solution(mesh):
    split = Mesh(mesh.devices.reshape(-1, X, C, Y), ("z", "x", "c", "y"))
    dp = ("z", "x", "c")
    return jax.shard_map(
        body,
        mesh=split,
        in_specs=(P(dp, "y", None), P(dp, None, "y"), P(), P(dp), P(), P()),
        out_specs=P(dp, "y"),
        check_vma=False,
    )
```

```python
import jax
import jax.numpy as jnp
from jax import lax
from jax.experimental import pallas as pl
from jax.experimental.pallas import tpu as pltpu
from jax.sharding import Mesh, PartitionSpec as P

X, C, Y = 4, 2, 8
CAP = 12
ROWS = 40
PER = ROWS // Y
BLK = 40
COLS = 448
LANES = 512
TOKENS = 64
VIRTUAL = 576
RAISE = 64.0
F32, BF16, F16 = jnp.float32, jnp.bfloat16, jnp.float16
VMEM = pl.BlockSpec(memory_space=pltpu.VMEM)
SMEM = pl.BlockSpec(memory_space=pltpu.SMEM)
ANY = pl.BlockSpec(memory_space=pl.ANY)
PARAMS = pltpu.CompilerParams(vmem_limit_bytes=16 * 1024 * 1024)
WIDE = pltpu.CompilerParams(vmem_limit_bytes=56 * 1024 * 1024)


def iota(shape, axis):
    return lax.broadcasted_iota(jnp.int32, shape, axis)


def steps(value, width, most):
    return sum((value >= width * i).astype(jnp.int32) for i in range(1, most))


def fetch(pairs, sems):
    copies = [pltpu.make_async_copy(src, dst, sems.at[i]) for i, (src, dst) in enumerate(pairs)]
    for one in copies:
        one.start()
    return copies


def prepare(zs, *refs):
    sources, (out_ref, scaled_ref, fullest_ref), held = refs[:6], refs[6:9], refs[9:15]
    sems = refs[15]
    act_ref, cot_ref, scales_ref, worker_ref, counts_ref, owned_ref = held
    copies = fetch(list(zip(sources, held)), sems)
    dp = (lax.axis_index("z") * X + lax.axis_index("x")) * C + lax.axis_index("c")
    slot = steps(iota((CAP * ROWS, 1), 0), ROWS, CAP)
    weight = jnp.zeros((CAP * ROWS, 1), F32)
    for one in copies[1:]:
        one.wait()
    count = counts_ref[dp]
    for s in range(CAP):
        looked_up = jnp.where(s < count, scales_ref[worker_ref[s]], 0.0)
        weight = jnp.where(slot == s, looked_up, weight)
    weight = weight / VIRTUAL
    scaled_ref[...] = (weight * cot_ref[...].astype(F32)).astype(BF16)

    def fuller(chip, most):
        return jnp.maximum(most, counts_ref[C * chip] + counts_ref[C * chip + 1])

    fullest_ref[0] = lax.fori_loop(0, counts_ref.shape[0] // C, fuller, 0)

    groups = -(-zs // 3)
    lane = iota((CAP, 128), 1)
    last = act_ref.shape[2] // 128 - 2
    copies[0].wait()

    def feature_block(f, carry):
        for g in range(groups):
            tiles = [jnp.zeros((CAP, 128), F32) for _ in range(PER)]
            for j in range(min(3, zs - 3 * g)):
                start = owned_ref[(3 * g + j) * X * C + f] * BLK
                tile = jnp.minimum(start // 128, last)
                shift = lax.rem(BLK * j - (start - tile * 128) + 256, 256)
                window = pl.ds(pl.multiple_of(tile * 128, 128), 256)
                keep = (lane >= BLK * j) & (lane < BLK * (j + 1))
                for t in range(PER):
                    rolled = pltpu.roll(act_ref[t, :, window].astype(F32), shift, 1)
                    tiles[t] = jnp.where(keep, rolled[:, :128], tiles[t])
            full = jnp.concatenate([*tiles, jnp.zeros((TOKENS - PER * CAP, 128), F32)], 0)
            out_ref[f, :, 128 * g : 128 * (g + 1)] = full.astype(BF16)
        return carry

    lax.fori_loop(0, X * C, feature_block, 0)


def pick(codes_out, codes_in):
    return jnp.where(codes_out == codes_in, 1.0, 0.0).astype(BF16)


def compact_act(wave, counts_hbm, got_ref, out_ref, counts_ref, sems):
    copies = fetch([(counts_hbm, counts_ref)], sems)
    base = lax.axis_index("z") * X * C
    m = iota((2 * TOKENS, 1), 0)
    half = (m >= TOKENS).astype(jnp.int32)
    row = m - TOKENS * half
    t = steps(row, CAP, 6)
    code_out = jnp.where(row < PER * CAP, half * 10000 + t * 100 + row - CAP * t, -2)
    k = iota((1, 2 * C * TOKENS), 1)
    block = steps(k, TOKENS, 2 * C)
    row = k - TOKENS * block
    t = steps(row, CAP, 6)
    s = row - CAP * t
    half = block >> 1
    core = block & 1
    for one in copies:
        one.wait()
    for p in range(X // 2):
        n = [counts_ref[base + 4 * p + i] for i in range(4)]
        live = jnp.where(
            half == 1, jnp.where(core == 1, n[3], n[2]), jnp.where(core == 1, n[1], n[0])
        )
        place = s + core * jnp.where(half == 1, n[2], n[0]) - CAP * wave
        there = (row < PER * CAP) & (s < live) & (place >= 0) & (place < CAP)
        code_in = jnp.where(there, half * 10000 + t * 100 + place, -1)
        got = got_ref[2 * C * p * TOKENS : 2 * C * (p + 1) * TOKENS, :]
        out = lax.dot_general(
            got, pick(code_out, code_in), (((0,), (1,)), ((), ())), preferred_element_type=F32
        )
        out_ref[:, 128 * p : 128 * (p + 1)] = out.astype(BF16)


def compact_cot(wave, counts_hbm, own_ref, other_ref, out_ref, counts_ref, sems):
    copies = fetch([(counts_hbm, counts_ref)], sems)
    base = (lax.axis_index("z") * X + lax.axis_index("x")) * C
    me = lax.axis_index("c")
    for one in copies:
        one.wait()
    first = counts_ref[base]
    k = iota((1, CAP * ROWS), 1)
    slot = steps(k, ROWS, CAP)
    row_in = k - ROWS * slot
    codes = []
    for core in (me, 1 - me):
        place = slot + core * first - CAP * wave
        there = (slot < counts_ref[base + core]) & (place >= 0) & (place < CAP)
        codes.append(jnp.where(there, row_in * 100 + place, -1))
    m = iota((2 * TOKENS, 1), 0)
    half = (m >= TOKENS).astype(jnp.int32)
    row = m - TOKENS * half
    t = steps(row, CAP, 6)
    for p in range(Y // 2):
        r = PER * (2 * p + half) + t
        code_out = jnp.where(row < PER * CAP, r * 100 + row - CAP * t, -2)
        out = jnp.dot(pick(code_out, codes[0]), own_ref[...], preferred_element_type=F32)
        out += jnp.dot(pick(code_out, codes[1]), other_ref[...], preferred_element_type=F32)
        full = jnp.concatenate([out, jnp.zeros((2 * TOKENS, LANES - COLS), F32)], 1)
        out_ref[2 * TOKENS * p : 2 * TOKENS * (p + 1), :] = full.astype(BF16)


def join(after_ref, one_ref, two_ref, out_ref, sems):
    rows = one_ref.shape[0]
    halves = [(one_ref, out_ref.at[0:rows]), (two_ref, out_ref.at[rows : 2 * rows])]
    for copy in fetch(halves, sems):
        copy.wait()


def multiply_near(begun, *refs):
    acts, (own, one, pair), rest = refs[:5], refs[5:8], refs[8 + begun :]
    out_ref, cot_ref, sems = rest
    x, y, c = lax.axis_index("x"), lax.axis_index("y"), lax.axis_index("c")
    near = 1 + 2 * c
    places = [
        (own, cot_ref.at[:, x]),
        (one, cot_ref.at[:, x ^ near]),
        (pair.at[0:Y], cot_ref.at[:, x ^ (4 - near)]),
        (pair.at[Y : 2 * Y], cot_ref.at[:, x ^ 2]),
    ]
    for copy in fetch(places, sems):
        copy.wait()
    total = refs[8][...] if begun else jnp.zeros(out_ref.shape, F32)
    out_ref[...] = total + outer(y, c, acts, (0, 1, -1, 2, -2), cot_ref)


def outer(y, c, acts, ks, cot_ref):
    total = jnp.zeros((acts[0].shape[0], LANES), F32)
    for k, ref in zip(ks, acts):
        cot = cot_ref[lax.rem(y - (1 - 2 * c) * k + Y, Y)].reshape(X * TOKENS, LANES)
        total += jnp.dot(ref[...], cot, preferred_element_type=F32)
    return total


def multiply_far(zs, last, *refs):
    acts, (cot_ref, total_ref, out_ref) = refs[:3], refs[3:]
    y, c = lax.axis_index("y"), lax.axis_index("c")
    total = total_ref[...] + outer(y, c, acts, (4, 3, -3), cot_ref)
    if not last:
        out_ref[...] = total
        return
    for z in range(zs):
        begin = 128 * (z // 3) + BLK * (z % 3)
        out_ref[z] = total[begin : begin + BLK, :COLS] * RAISE


def body(*inputs):
    term, fullest = partial_sums(*inputs)
    term = lax.cond(
        fullest > CAP, lambda done, *again: partial_sums(*again, waves=C)[0], lambda done, *_: done,
        term, *inputs,
    )
    parts = lax.all_to_all(term, "z", 0, 0, tiled=True)
    return jnp.sum(parts.astype(F32) * (1.0 / RAISE), axis=0)


def partial_sums(
    activations, cotangent, scales, slot_worker, slot_counts, owned_block, waves=1
):
    zs = lax.axis_size("z")
    features = 128 * (-(-zs // 3))
    shape = jax.ShapeDtypeStruct
    act = jnp.transpose(activations, (1, 0, 2))
    cot = cotangent.reshape(CAP * ROWS, COLS)
    inputs = (act, cot, scales, slot_worker, slot_counts, owned_block)
    sent, scaled, fullest = pl.pallas_call(
        lambda *refs: prepare(zs, *refs),
        out_shape=(
            pltpu.VMEM((X * C, TOKENS, features), BF16),
            pltpu.VMEM(cot.shape, BF16),
            shape((1,), jnp.int32),
        ),
        in_specs=[ANY] * 6,
        out_specs=(VMEM, VMEM, SMEM),
        scratch_shapes=[
            *[pltpu.VMEM(a.shape, a.dtype) for a in inputs[:2]],
            *[pltpu.SMEM(a.shape, a.dtype) for a in inputs[2:]],
            pltpu.SemaphoreType.DMA((6,)),
        ],
        compiler_params=WIDE,
    )(*inputs)
    got = lax.all_to_all(sent, ("x", "c"), 0, 0, tiled=True).reshape(X * C * TOKENS, features)
    other = lax.ppermute(scaled, "c", [(0, 1), (1, 0)])
    counts_scratch = [
        pltpu.SMEM(slot_counts.shape, jnp.int32),
        pltpu.SemaphoreType.DMA((1,)),
    ]

    def shifted(array, by):
        pairs = [
            (c * Y + y, c * Y + (y + by * (1 - 2 * c)) % Y) for c in range(C) for y in range(Y)
        ]
        return lax.ppermute(array, ("c", "y"), pairs)

    def swapped(array, by):
        pairs = [(x * C + c, (x ^ by[c]) * C + c) for x in range(X) for c in range(C)]
        return lax.ppermute(array, ("x", "c"), pairs)

    def product(near, far, cots, total, last):
        begun = [] if total is None else [total]
        sums = shape((features, LANES), F32)
        total, laid = pl.pallas_call(
            lambda *refs: multiply_near(len(begun), *refs),
            out_shape=(sums, shape((Y, X, TOKENS, LANES), BF16)),
            in_specs=[VMEM] * 5 + [ANY] * 3 + [VMEM] * len(begun),
            out_specs=(VMEM, VMEM),
            scratch_shapes=[pltpu.SemaphoreType.DMA((X,))],
            compiler_params=PARAMS,
        )(*near, *cots, *begun)
        return pl.pallas_call(
            lambda *refs: multiply_far(zs, last, *refs),
            out_shape=shape((zs, BLK, COLS), F32) if last else sums,
            in_specs=[VMEM] * 5,
            out_specs=VMEM,
            compiler_params=PARAMS,
        )(*far, laid, total)

    total = None
    for wave in range(waves):
        unit = pl.pallas_call(
            lambda *refs: compact_act(wave, *refs),
            out_shape=shape((features, X * TOKENS), BF16),
            in_specs=[ANY, VMEM],
            out_specs=VMEM,
            scratch_shapes=counts_scratch,
            compiler_params=PARAMS,
        )(slot_counts, got)
        chip = pl.pallas_call(
            lambda *refs: compact_cot(wave, *refs),
            out_shape=shape((Y * TOKENS, LANES), BF16),
            in_specs=[ANY, VMEM, VMEM],
            out_specs=VMEM,
            scratch_shapes=counts_scratch,
            compiler_params=PARAMS,
        )(slot_counts, scaled, other)
        one = swapped(chip, (1, 3))
        ahead, behind = shifted(unit, 2), shifted(unit, -2)
        near = [shifted(unit, 1), shifted(unit, -1)]
        far = [shifted(ahead, 2), shifted(ahead, 1), shifted(behind, -1)]
        both = pl.pallas_call(
            join,
            out_shape=shape((2 * chip.shape[0], LANES), BF16),
            in_specs=[ANY, ANY, ANY],
            out_specs=ANY,
            scratch_shapes=[pltpu.SemaphoreType.DMA((2,))],
            compiler_params=PARAMS,
        )(near[0], chip, one)
        pair = swapped(both, (3, 1))
        cots = [c.reshape(-1, TOKENS, LANES) for c in (chip, one, pair)]
        total = product([unit, *near, ahead, behind], far, cots, total, wave == waves - 1)
    return total.astype(F16), fullest[0]


def solution(mesh):
    split = Mesh(mesh.devices.reshape(-1, X, C, Y), ("z", "x", "c", "y"))
    dp = ("z", "x", "c")
    return jax.shard_map(
        body,
        mesh=split,
        in_specs=(P(dp, "y", None), P(dp, None, "y"), P(), P(dp), P(), P()),
        out_specs=P(dp, "y"),
        check_vma=False,
    )
```

```python
import jax
import jax.numpy as jnp
from jax import lax
from jax.experimental import pallas as pl
from jax.experimental.pallas import tpu as pltpu
from jax.sharding import Mesh, PartitionSpec as P

X, C, Y = 4, 2, 8
CAP = 12
ROWS = 40
PER = ROWS // Y
BLK = 40
COLS = 448
LANES = 512
TOKENS = 64
VIRTUAL = 576
RAISE = 64.0
F32, BF16, F16 = jnp.float32, jnp.bfloat16, jnp.float16
VMEM = pl.BlockSpec(memory_space=pltpu.VMEM)
SMEM = pl.BlockSpec(memory_space=pltpu.SMEM)
ANY = pl.BlockSpec(memory_space=pl.ANY)
PARAMS = pltpu.CompilerParams(vmem_limit_bytes=16 * 1024 * 1024)
WIDE = pltpu.CompilerParams(vmem_limit_bytes=56 * 1024 * 1024)


def iota(shape, axis):
    return lax.broadcasted_iota(jnp.int32, shape, axis)


def steps(value, width, most):
    return sum((value >= width * i).astype(jnp.int32) for i in range(1, most))


def fetch(pairs, sems):
    copies = [pltpu.make_async_copy(src, dst, sems.at[i]) for i, (src, dst) in enumerate(pairs)]
    for one in copies:
        one.start()
    return copies


def prepare(zs, *refs):
    sources, (out_ref, scaled_ref, fullest_ref), held = refs[:6], refs[6:9], refs[9:15]
    sems = refs[15]
    act_ref, cot_ref, scales_ref, worker_ref, counts_ref, owned_ref = held
    copies = fetch(list(zip(sources, held)), sems)
    dp = (lax.axis_index("z") * X + lax.axis_index("x")) * C + lax.axis_index("c")
    slot = steps(iota((CAP * ROWS, 1), 0), ROWS, CAP)
    weight = jnp.zeros((CAP * ROWS, 1), F32)
    for one in copies[1:]:
        one.wait()
    count = counts_ref[dp]
    for s in range(CAP):
        looked_up = jnp.where(s < count, scales_ref[worker_ref[s]], 0.0)
        weight = jnp.where(slot == s, looked_up, weight)
    weight = weight / VIRTUAL
    scaled_ref[...] = (weight * cot_ref[...].astype(F32)).astype(BF16)

    def fuller(chip, most):
        return jnp.maximum(most, counts_ref[C * chip] + counts_ref[C * chip + 1])

    fullest_ref[0] = lax.fori_loop(0, counts_ref.shape[0] // C, fuller, 0)

    groups = -(-zs // 3)
    lane = iota((CAP, 128), 1)
    last = act_ref.shape[2] // 128 - 2
    copies[0].wait()

    def feature_block(f, carry):
        for g in range(groups):
            tiles = [jnp.zeros((CAP, 128), F32) for _ in range(PER)]
            for j in range(min(3, zs - 3 * g)):
                start = owned_ref[(3 * g + j) * X * C + f] * BLK
                tile = jnp.minimum(start // 128, last)
                shift = lax.rem(BLK * j - (start - tile * 128) + 256, 256)
                window = pl.ds(pl.multiple_of(tile * 128, 128), 256)
                keep = (lane >= BLK * j) & (lane < BLK * (j + 1))
                for t in range(PER):
                    rolled = pltpu.roll(act_ref[t, :, window].astype(F32), shift, 1)
                    tiles[t] = jnp.where(keep, rolled[:, :128], tiles[t])
            full = jnp.concatenate([*tiles, jnp.zeros((TOKENS - PER * CAP, 128), F32)], 0)
            out_ref[f, :, 128 * g : 128 * (g + 1)] = full.astype(BF16)
        return carry

    lax.fori_loop(0, X * C, feature_block, 0)


def pick(codes_out, codes_in):
    return jnp.where(codes_out == codes_in, 1.0, 0.0).astype(BF16)


def compact_act(zs, wave, counts_hbm, got_ref, out_ref, counts_ref, sems):
    copies = fetch([(counts_hbm, counts_ref)], sems)
    base = lax.axis_index("z") * X * C
    m = iota((2 * TOKENS, 1), 0)
    half = (m >= TOKENS).astype(jnp.int32)
    row = m - TOKENS * half
    t = steps(row, CAP, 6)
    code_out = jnp.where(row < PER * CAP, half * 10000 + t * 100 + row - CAP * t, -2)
    k = iota((1, 2 * C * TOKENS), 1)
    block = steps(k, TOKENS, 2 * C)
    row = k - TOKENS * block
    t = steps(row, CAP, 6)
    s = row - CAP * t
    half = block >> 1
    core = block & 1
    for one in copies:
        one.wait()
    for p in range(X // 2):
        n = [counts_ref[base + 4 * p + i] for i in range(4)]
        live = jnp.where(
            half == 1, jnp.where(core == 1, n[3], n[2]), jnp.where(core == 1, n[1], n[0])
        )
        place = s + core * jnp.where(half == 1, n[2], n[0]) - CAP * wave
        there = (row < PER * CAP) & (s < live) & (place >= 0) & (place < CAP)
        code_in = jnp.where(there, half * 10000 + t * 100 + place, -1)
        got = got_ref[2 * C * p * TOKENS : 2 * C * (p + 1) * TOKENS, :]
        out = lax.dot_general(
            got, pick(code_out, code_in), (((0,), (1,)), ((), ())), preferred_element_type=F32
        )
        rows = [out[128 * g : 128 * g + BLK * min(3, zs - 3 * g)] for g in range(-(-zs // 3))]
        out_ref[:, 128 * p : 128 * (p + 1)] = jnp.concatenate(rows, 0).astype(BF16)


def compact_cot(wave, counts_hbm, own_ref, other_ref, out_ref, counts_ref, sems):
    copies = fetch([(counts_hbm, counts_ref)], sems)
    base = (lax.axis_index("z") * X + lax.axis_index("x")) * C
    me = lax.axis_index("c")
    for one in copies:
        one.wait()
    first = counts_ref[base]
    k = iota((1, CAP * ROWS), 1)
    slot = steps(k, ROWS, CAP)
    row_in = k - ROWS * slot
    codes = []
    for core in (me, 1 - me):
        place = slot + core * first - CAP * wave
        there = (slot < counts_ref[base + core]) & (place >= 0) & (place < CAP)
        codes.append(jnp.where(there, row_in * 100 + place, -1))
    m = iota((2 * TOKENS, 1), 0)
    half = (m >= TOKENS).astype(jnp.int32)
    row = m - TOKENS * half
    t = steps(row, CAP, 6)
    for p in range(Y // 2):
        r = PER * (2 * p + half) + t
        code_out = jnp.where(row < PER * CAP, r * 100 + row - CAP * t, -2)
        out = jnp.dot(pick(code_out, codes[0]), own_ref[...], preferred_element_type=F32)
        out += jnp.dot(pick(code_out, codes[1]), other_ref[...], preferred_element_type=F32)
        full = jnp.concatenate([out, jnp.zeros((2 * TOKENS, LANES - COLS), F32)], 1)
        out_ref[2 * TOKENS * p : 2 * TOKENS * (p + 1), :] = full.astype(BF16)


def join(after_ref, one_ref, two_ref, out_ref, sems):
    rows = one_ref.shape[0]
    halves = [(one_ref, out_ref.at[0:rows]), (two_ref, out_ref.at[rows : 2 * rows])]
    for copy in fetch(halves, sems):
        copy.wait()


def multiply_near(begun, *refs):
    acts, (own, one, pair), rest = refs[:5], refs[5:8], refs[8 + begun :]
    out_ref, cot_ref, sems = rest
    x, y, c = lax.axis_index("x"), lax.axis_index("y"), lax.axis_index("c")
    near = 1 + 2 * c
    places = [
        (own, cot_ref.at[:, x]),
        (one, cot_ref.at[:, x ^ near]),
        (pair.at[0:Y], cot_ref.at[:, x ^ (4 - near)]),
        (pair.at[Y : 2 * Y], cot_ref.at[:, x ^ 2]),
    ]
    for copy in fetch(places, sems):
        copy.wait()
    total = refs[8][...] if begun else jnp.zeros(out_ref.shape, F32)
    out_ref[...] = total + outer(y, c, acts, (0, 1, -1, 2, -2), cot_ref)


def outer(y, c, acts, ks, cot_ref):
    total = jnp.zeros((acts[0].shape[0], LANES), F32)
    for k, ref in zip(ks, acts):
        cot = cot_ref[lax.rem(y - (1 - 2 * c) * k + Y, Y)].reshape(X * TOKENS, LANES)
        total += jnp.dot(ref[...], cot, preferred_element_type=F32)
    return total


def multiply_far(zs, last, *refs):
    acts, (cot_ref, total_ref, out_ref) = refs[:3], refs[3:]
    y, c = lax.axis_index("y"), lax.axis_index("c")
    total = total_ref[...] + outer(y, c, acts, (4, 3, -3), cot_ref)
    if not last:
        out_ref[...] = total
        return
    for z in range(zs):
        out_ref[z] = total[BLK * z : BLK * (z + 1), :COLS] * RAISE


def body(*inputs):
    term, fullest = partial_sums(*inputs)
    term = lax.cond(
        fullest > CAP, lambda done, *again: partial_sums(*again, waves=C)[0], lambda done, *_: done,
        term, *inputs,
    )
    parts = lax.all_to_all(term, "z", 0, 0, tiled=True)
    return jnp.sum(parts.astype(F32) * (1.0 / RAISE), axis=0)


def partial_sums(
    activations, cotangent, scales, slot_worker, slot_counts, owned_block, waves=1
):
    zs = lax.axis_size("z")
    features = 128 * (-(-zs // 3))
    shape = jax.ShapeDtypeStruct
    act = jnp.transpose(activations, (1, 0, 2))
    cot = cotangent.reshape(CAP * ROWS, COLS)
    inputs = (act, cot, scales, slot_worker, slot_counts, owned_block)
    sent, scaled, fullest = pl.pallas_call(
        lambda *refs: prepare(zs, *refs),
        out_shape=(
            pltpu.VMEM((X * C, TOKENS, features), BF16),
            pltpu.VMEM(cot.shape, BF16),
            shape((1,), jnp.int32),
        ),
        in_specs=[ANY] * 6,
        out_specs=(VMEM, VMEM, SMEM),
        scratch_shapes=[
            *[pltpu.VMEM(a.shape, a.dtype) for a in inputs[:2]],
            *[pltpu.SMEM(a.shape, a.dtype) for a in inputs[2:]],
            pltpu.SemaphoreType.DMA((6,)),
        ],
        compiler_params=WIDE,
    )(*inputs)
    got = lax.all_to_all(sent, ("x", "c"), 0, 0, tiled=True).reshape(X * C * TOKENS, features)
    other = lax.ppermute(scaled, "c", [(0, 1), (1, 0)])
    counts_scratch = [
        pltpu.SMEM(slot_counts.shape, jnp.int32),
        pltpu.SemaphoreType.DMA((1,)),
    ]

    def shifted(array, by):
        pairs = [
            (c * Y + y, c * Y + (y + by * (1 - 2 * c)) % Y) for c in range(C) for y in range(Y)
        ]
        return lax.ppermute(array, ("c", "y"), pairs)

    def swapped(array, by):
        pairs = [(x * C + c, (x ^ by[c]) * C + c) for x in range(X) for c in range(C)]
        return lax.ppermute(array, ("x", "c"), pairs)

    def product(near, far, cots, total, last):
        begun = [] if total is None else [total]
        sums = shape((BLK * zs, LANES), F32)
        total, laid = pl.pallas_call(
            lambda *refs: multiply_near(len(begun), *refs),
            out_shape=(sums, shape((Y, X, TOKENS, LANES), BF16)),
            in_specs=[VMEM] * 5 + [ANY] * 3 + [VMEM] * len(begun),
            out_specs=(VMEM, VMEM),
            scratch_shapes=[pltpu.SemaphoreType.DMA((X,))],
            compiler_params=PARAMS,
        )(*near, *cots, *begun)
        return pl.pallas_call(
            lambda *refs: multiply_far(zs, last, *refs),
            out_shape=shape((zs, BLK, COLS), F32) if last else sums,
            in_specs=[VMEM] * 5,
            out_specs=VMEM,
            compiler_params=PARAMS,
        )(*far, laid, total)

    total = None
    for wave in range(waves):
        unit = pl.pallas_call(
            lambda *refs: compact_act(zs, wave, *refs),
            out_shape=shape((BLK * zs, X * TOKENS), BF16),
            in_specs=[ANY, VMEM],
            out_specs=VMEM,
            scratch_shapes=counts_scratch,
            compiler_params=PARAMS,
        )(slot_counts, got)
        chip = pl.pallas_call(
            lambda *refs: compact_cot(wave, *refs),
            out_shape=shape((Y * TOKENS, LANES), BF16),
            in_specs=[ANY, VMEM, VMEM],
            out_specs=VMEM,
            scratch_shapes=counts_scratch,
            compiler_params=PARAMS,
        )(slot_counts, scaled, other)
        one = swapped(chip, (1, 3))
        ahead, behind = shifted(unit, 2), shifted(unit, -2)
        near = [shifted(unit, 1), shifted(unit, -1)]
        far = [shifted(ahead, 2), shifted(ahead, 1), shifted(behind, -1)]
        both = pl.pallas_call(
            join,
            out_shape=shape((2 * chip.shape[0], LANES), BF16),
            in_specs=[ANY, ANY, ANY],
            out_specs=ANY,
            scratch_shapes=[pltpu.SemaphoreType.DMA((2,))],
            compiler_params=PARAMS,
        )(near[0], chip, one)
        pair = swapped(both, (3, 1))
        cots = [c.reshape(-1, TOKENS, LANES) for c in (chip, one, pair)]
        total = product([unit, *near, ahead, behind], far, cots, total, wave == waves - 1)
    return total.astype(F16), fullest[0]


def solution(mesh):
    split = Mesh(mesh.devices.reshape(-1, X, C, Y), ("z", "x", "c", "y"))
    dp = ("z", "x", "c")
    return jax.shard_map(
        body,
        mesh=split,
        in_specs=(P(dp, "y", None), P(dp, None, "y"), P(), P(dp), P(), P()),
        out_specs=P(dp, "y"),
        check_vma=False,
    )
```

```python
import jax
import jax.numpy as jnp
from jax import lax
from jax.experimental import pallas as pl
from jax.experimental.pallas import tpu as pltpu
from jax.sharding import Mesh, PartitionSpec as P

X, C, Y = 4, 2, 8
CAP = 12
ROWS = 40
PER = ROWS // Y
BLK = 40
COLS = 448
LANES = 512
TOKENS = 64
VIRTUAL = 576
RAISE = 64.0
F32, BF16, F16 = jnp.float32, jnp.bfloat16, jnp.float16
VMEM = pl.BlockSpec(memory_space=pltpu.VMEM)
SMEM = pl.BlockSpec(memory_space=pltpu.SMEM)
ANY = pl.BlockSpec(memory_space=pl.ANY)
PARAMS = pltpu.CompilerParams(vmem_limit_bytes=16 * 1024 * 1024)
WIDE = pltpu.CompilerParams(vmem_limit_bytes=56 * 1024 * 1024)


def iota(shape, axis):
    return lax.broadcasted_iota(jnp.int32, shape, axis)


def steps(value, width, most):
    return sum((value >= width * i).astype(jnp.int32) for i in range(1, most))


def fetch(pairs, sems):
    copies = [pltpu.make_async_copy(src, dst, sems.at[i]) for i, (src, dst) in enumerate(pairs)]
    for one in copies:
        one.start()
    return copies


def prepare(zs, *refs):
    sources, (out_ref, scaled_ref, fullest_ref), held = refs[:6], refs[6:9], refs[9:15]
    sems = refs[15]
    act_ref, cot_ref, scales_ref, worker_ref, counts_ref, owned_ref = held
    copies = fetch(list(zip(sources, held)), sems)
    dp = (lax.axis_index("z") * X + lax.axis_index("x")) * C + lax.axis_index("c")
    slot = steps(iota((CAP * ROWS, 1), 0), ROWS, CAP)
    weight = jnp.zeros((CAP * ROWS, 1), F32)
    for one in copies[1:]:
        one.wait()
    count = counts_ref[dp]
    for s in range(CAP):
        looked_up = jnp.where(s < count, scales_ref[worker_ref[s]], 0.0)
        weight = jnp.where(slot == s, looked_up, weight)
    weight = weight / VIRTUAL
    scaled_ref[...] = (weight * cot_ref[...].astype(F32)).astype(BF16)

    def fuller(chip, most):
        return jnp.maximum(most, counts_ref[C * chip] + counts_ref[C * chip + 1])

    fullest_ref[0] = lax.fori_loop(0, counts_ref.shape[0] // C, fuller, 0)

    groups = -(-zs // 3)
    lane = iota((CAP, 128), 1)
    last = act_ref.shape[2] // 128 - 2
    copies[0].wait()

    def feature_block(f, carry):
        for g in range(groups):
            tiles = [jnp.zeros((CAP, 128), F32) for _ in range(PER)]
            for j in range(min(3, zs - 3 * g)):
                start = owned_ref[(3 * g + j) * X * C + f] * BLK
                tile = jnp.minimum(start // 128, last)
                shift = lax.rem(BLK * j - (start - tile * 128) + 256, 256)
                window = pl.ds(pl.multiple_of(tile * 128, 128), 256)
                keep = (lane >= BLK * j) & (lane < BLK * (j + 1))
                for t in range(PER):
                    rolled = pltpu.roll(act_ref[t, :, window].astype(F32), shift, 1)
                    tiles[t] = jnp.where(keep, rolled[:, :128], tiles[t])
            full = jnp.concatenate([*tiles, jnp.zeros((TOKENS - PER * CAP, 128), F32)], 0)
            out_ref[f, :, 128 * g : 128 * (g + 1)] = full.astype(BF16)
        return carry

    lax.fori_loop(0, X * C, feature_block, 0, unroll=2)


def pick(codes_out, codes_in):
    return jnp.where(codes_out == codes_in, 1.0, 0.0).astype(BF16)


def compact_act(zs, wave, counts_hbm, got_ref, out_ref, counts_ref, sems):
    copies = fetch([(counts_hbm, counts_ref)], sems)
    base = lax.axis_index("z") * X * C
    m = iota((2 * TOKENS, 1), 0)
    half = (m >= TOKENS).astype(jnp.int32)
    row = m - TOKENS * half
    t = steps(row, CAP, 6)
    code_out = jnp.where(row < PER * CAP, half * 10000 + t * 100 + row - CAP * t, -2)
    k = iota((1, 2 * C * TOKENS), 1)
    block = steps(k, TOKENS, 2 * C)
    row = k - TOKENS * block
    t = steps(row, CAP, 6)
    s = row - CAP * t
    half = block >> 1
    core = block & 1
    for one in copies:
        one.wait()
    for p in range(X // 2):
        n = [counts_ref[base + 4 * p + i] for i in range(4)]
        live = jnp.where(
            half == 1, jnp.where(core == 1, n[3], n[2]), jnp.where(core == 1, n[1], n[0])
        )
        place = s + core * jnp.where(half == 1, n[2], n[0]) - CAP * wave
        there = (row < PER * CAP) & (s < live) & (place >= 0) & (place < CAP)
        code_in = jnp.where(there, half * 10000 + t * 100 + place, -1)
        got = got_ref[2 * C * p * TOKENS : 2 * C * (p + 1) * TOKENS, :]
        out = lax.dot_general(
            got, pick(code_out, code_in), (((0,), (1,)), ((), ())), preferred_element_type=F32
        )
        rows = [out[128 * g : 128 * g + BLK * min(3, zs - 3 * g)] for g in range(-(-zs // 3))]
        out_ref[:, 128 * p : 128 * (p + 1)] = jnp.concatenate(rows, 0).astype(BF16)


def compact_cot(wave, counts_hbm, own_ref, other_ref, out_ref, counts_ref, sems):
    copies = fetch([(counts_hbm, counts_ref)], sems)
    base = (lax.axis_index("z") * X + lax.axis_index("x")) * C
    me = lax.axis_index("c")
    for one in copies:
        one.wait()
    first = counts_ref[base]
    k = iota((1, CAP * ROWS), 1)
    slot = steps(k, ROWS, CAP)
    row_in = k - ROWS * slot
    codes = []
    for core in (me, 1 - me):
        place = slot + core * first - CAP * wave
        there = (slot < counts_ref[base + core]) & (place >= 0) & (place < CAP)
        codes.append(jnp.where(there, row_in * 100 + place, -1))
    m = iota((2 * TOKENS, 1), 0)
    half = (m >= TOKENS).astype(jnp.int32)
    row = m - TOKENS * half
    t = steps(row, CAP, 6)
    for p in range(Y // 2):
        r = PER * (2 * p + half) + t
        code_out = jnp.where(row < PER * CAP, r * 100 + row - CAP * t, -2)
        out = jnp.dot(pick(code_out, codes[0]), own_ref[...], preferred_element_type=F32)
        out += jnp.dot(pick(code_out, codes[1]), other_ref[...], preferred_element_type=F32)
        full = jnp.concatenate([out, jnp.zeros((2 * TOKENS, LANES - COLS), F32)], 1)
        out_ref[2 * TOKENS * p : 2 * TOKENS * (p + 1), :] = full.astype(BF16)


def join(after_ref, one_ref, two_ref, out_ref, sems):
    rows = one_ref.shape[0]
    halves = [(one_ref, out_ref.at[0:rows]), (two_ref, out_ref.at[rows : 2 * rows])]
    for copy in fetch(halves, sems):
        copy.wait()


def multiply_near(begun, *refs):
    acts, (own, one, pair), rest = refs[:5], refs[5:8], refs[8 + begun :]
    out_ref, cot_ref, sems = rest
    x, y, c = lax.axis_index("x"), lax.axis_index("y"), lax.axis_index("c")
    near = 1 + 2 * c
    places = [
        (own, cot_ref.at[:, x]),
        (one, cot_ref.at[:, x ^ near]),
        (pair.at[0:Y], cot_ref.at[:, x ^ (4 - near)]),
        (pair.at[Y : 2 * Y], cot_ref.at[:, x ^ 2]),
    ]
    for copy in fetch(places, sems):
        copy.wait()
    total = refs[8][...] if begun else jnp.zeros(out_ref.shape, F32)
    out_ref[...] = total + outer(y, c, acts, (0, 1, -1, 2, -2), cot_ref)


def outer(y, c, acts, ks, cot_ref):
    total = jnp.zeros((acts[0].shape[0], LANES), F32)
    for k, ref in zip(ks, acts):
        cot = cot_ref[lax.rem(y - (1 - 2 * c) * k + Y, Y)].reshape(X * TOKENS, LANES)
        total += jnp.dot(ref[...], cot, preferred_element_type=F32)
    return total


def multiply_far(zs, last, *refs):
    acts, (cot_ref, total_ref, out_ref) = refs[:3], refs[3:]
    y, c = lax.axis_index("y"), lax.axis_index("c")
    total = total_ref[...] + outer(y, c, acts, (4, 3, -3), cot_ref)
    if not last:
        out_ref[...] = total
        return
    for z in range(zs):
        out_ref[z] = total[BLK * z : BLK * (z + 1), :COLS] * RAISE


def body(*inputs):
    term, fullest = partial_sums(*inputs)
    term = lax.cond(
        fullest > CAP, lambda done, *again: partial_sums(*again, waves=C)[0], lambda done, *_: done,
        term, *inputs,
    )
    parts = lax.all_to_all(term, "z", 0, 0, tiled=True)
    return jnp.sum(parts.astype(F32) * (1.0 / RAISE), axis=0)


def partial_sums(
    activations, cotangent, scales, slot_worker, slot_counts, owned_block, waves=1
):
    zs = lax.axis_size("z")
    features = 128 * (-(-zs // 3))
    shape = jax.ShapeDtypeStruct
    act = jnp.transpose(activations, (1, 0, 2))
    cot = cotangent.reshape(CAP * ROWS, COLS)
    inputs = (act, cot, scales, slot_worker, slot_counts, owned_block)
    sent, scaled, fullest = pl.pallas_call(
        lambda *refs: prepare(zs, *refs),
        out_shape=(
            pltpu.VMEM((X * C, TOKENS, features), BF16),
            pltpu.VMEM(cot.shape, BF16),
            shape((1,), jnp.int32),
        ),
        in_specs=[ANY] * 6,
        out_specs=(VMEM, VMEM, SMEM),
        scratch_shapes=[
            *[pltpu.VMEM(a.shape, a.dtype) for a in inputs[:2]],
            *[pltpu.SMEM(a.shape, a.dtype) for a in inputs[2:]],
            pltpu.SemaphoreType.DMA((6,)),
        ],
        compiler_params=WIDE,
    )(*inputs)
    got = lax.all_to_all(sent, ("x", "c"), 0, 0, tiled=True).reshape(X * C * TOKENS, features)
    other = lax.ppermute(scaled, "c", [(0, 1), (1, 0)])
    counts_scratch = [
        pltpu.SMEM(slot_counts.shape, jnp.int32),
        pltpu.SemaphoreType.DMA((1,)),
    ]

    def shifted(array, by):
        pairs = [
            (c * Y + y, c * Y + (y + by * (1 - 2 * c)) % Y) for c in range(C) for y in range(Y)
        ]
        return lax.ppermute(array, ("c", "y"), pairs)

    def swapped(array, by):
        pairs = [(x * C + c, (x ^ by[c]) * C + c) for x in range(X) for c in range(C)]
        return lax.ppermute(array, ("x", "c"), pairs)

    def product(near, far, cots, total, last):
        begun = [] if total is None else [total]
        sums = shape((BLK * zs, LANES), F32)
        total, laid = pl.pallas_call(
            lambda *refs: multiply_near(len(begun), *refs),
            out_shape=(sums, shape((Y, X, TOKENS, LANES), BF16)),
            in_specs=[VMEM] * 5 + [ANY] * 3 + [VMEM] * len(begun),
            out_specs=(VMEM, VMEM),
            scratch_shapes=[pltpu.SemaphoreType.DMA((X,))],
            compiler_params=PARAMS,
        )(*near, *cots, *begun)
        return pl.pallas_call(
            lambda *refs: multiply_far(zs, last, *refs),
            out_shape=shape((zs, BLK, COLS), F32) if last else sums,
            in_specs=[VMEM] * 5,
            out_specs=VMEM,
            compiler_params=PARAMS,
        )(*far, laid, total)

    total = None
    for wave in range(waves):
        unit = pl.pallas_call(
            lambda *refs: compact_act(zs, wave, *refs),
            out_shape=shape((BLK * zs, X * TOKENS), BF16),
            in_specs=[ANY, VMEM],
            out_specs=VMEM,
            scratch_shapes=counts_scratch,
            compiler_params=PARAMS,
        )(slot_counts, got)
        chip = pl.pallas_call(
            lambda *refs: compact_cot(wave, *refs),
            out_shape=shape((Y * TOKENS, LANES), BF16),
            in_specs=[ANY, VMEM, VMEM],
            out_specs=VMEM,
            scratch_shapes=counts_scratch,
            compiler_params=PARAMS,
        )(slot_counts, scaled, other)
        one = swapped(chip, (1, 3))
        ahead, behind = shifted(unit, 2), shifted(unit, -2)
        near = [shifted(unit, 1), shifted(unit, -1)]
        far = [shifted(ahead, 2), shifted(ahead, 1), shifted(behind, -1)]
        both = pl.pallas_call(
            join,
            out_shape=shape((2 * chip.shape[0], LANES), BF16),
            in_specs=[ANY, ANY, ANY],
            out_specs=ANY,
            scratch_shapes=[pltpu.SemaphoreType.DMA((2,))],
            compiler_params=PARAMS,
        )(near[0], chip, one)
        pair = swapped(both, (3, 1))
        cots = [c.reshape(-1, TOKENS, LANES) for c in (chip, one, pair)]
        total = product([unit, *near, ahead, behind], far, cots, total, wave == waves - 1)
    return total.astype(F16), fullest[0]


def solution(mesh):
    split = Mesh(mesh.devices.reshape(-1, X, C, Y), ("z", "x", "c", "y"))
    dp = ("z", "x", "c")
    return jax.shard_map(
        body,
        mesh=split,
        in_specs=(P(dp, "y", None), P(dp, None, "y"), P(), P(dp), P(), P()),
        out_specs=P(dp, "y"),
        check_vma=False,
    )
```
